256 devices in a mesh: seq: 16 (over y, x_hi, core), grp: 16 (over x_lo, z).
Axes of the slice: x: 4 (x_hi: 2, x_lo: 2; x = x_hi * 2 + x_lo), y: 4, z: 8, core: 2. Of those that a mesh axis runs over, the one named last changes fastest.
Arguments:
- video_qkv: bfloat16 [3, 2048, 2048], P(None, 'seq', 'grp'), may hold values from -13 to 13
- audio_qkv: bfloat16 [3, 1024, 2048], P(None, 'seq', 'grp'), may hold values from -13 to 13
- head_slopes: float32 [16], P('grp'), may hold values from 0.05 to 0.8
- audio_frame: int32 [1024], replicated, may hold values from 0 to 31, as said below
- out_weight: bfloat16 [2048, 3072], P('grp'), may hold values from -0.125 to 0.125
- video_cot: bfloat16 [2048, 3072], P('seq', 'grp'), may hold values from -6 to 6
- audio_cot: bfloat16 [1024, 2048], P('seq', 'grp'), may hold values from -6 to 6
Outputs:
- video_out: bfloat16 [2048, 3072], P('seq', 'grp')
- audio_mix: bfloat16 [1024, 2048], P('seq', 'grp')
- video_grad: bfloat16 [3, 2048, 2048], P(None, 'seq', 'grp')
- audio_grad: bfloat16 [3, 1024, 2048], P(None, 'seq', 'grp')
The draws below stay inside these ranges and needn't reach their ends.
Inputs may be any that keep to these rules, and one draw needn't show every extreme that they name: `audio_frame`: audio token a lies within two frames of frame a * 32 // 1024; the first audio token lies in frame 0 and the last in frame 32 - 1.
All inputs are finite; a program needn't handle non-finite values.
Results may differ from the reference program's by a relative error of at most 0.035.
Values may be sent and summed in bfloat16 or wider, within the bound.
A program may use at most 64 MiB of HBM per device.

```python
import math
import jax
import jax.numpy as jnp
from jax import lax

D = 3072
HEAD_DIM = 128
TOK_DEV = 128
HEADS = 16
VIDEO = 2048
AUDIO = 1024
FRAME_TOK = 64
FRAMES = 32
N_SEQ = 16


def draw_video_qkv(key, part):
    key = jax.random.fold_in(key, 11)
    row_count = VIDEO
    col_count = HEADS * HEAD_DIM
    scaling = jnp.array([1.6, 1.6, 1.0], jnp.float32)[:, None, None]
    values = jax.random.truncated_normal(key, -3.5, 3.5, (3, row_count, col_count), jnp.float32) * scaling
    return values.astype(jnp.bfloat16)


def draw_audio_qkv(key, part):
    key = jax.random.fold_in(key, 17)
    row_count = AUDIO
    col_count = HEADS * HEAD_DIM
    scaling = jnp.array([1.6, 1.6, 1.0], jnp.float32)[:, None, None]
    values = jax.random.truncated_normal(key, -3.5, 3.5, (3, row_count, col_count), jnp.float32) * scaling
    return values.astype(jnp.bfloat16)


def draw_audio_frame(key, part):
    key = jax.random.fold_in(key, 23)
    position = jnp.arange(AUDIO, dtype=jnp.int32)
    nominal = position * FRAMES // AUDIO
    jitter = jax.random.randint(key, (AUDIO,), -2, 3, dtype=jnp.int32)
    frames = jnp.clip(nominal + jitter, 0, FRAMES - 1)
    frames = frames.at[0].set(0).at[AUDIO - 1].set(FRAMES - 1)
    return frames.astype(jnp.int32)


def shard_levels(own_key, dims, shards, low, top_value):
    loudness = 1.0
    for axis_at, blocks in shards:
        heights = jax.random.uniform(jax.random.fold_in(jax.random.fold_in(own_key, 6), axis_at), (blocks,), jnp.float32, low / len(shards), top_value / len(shards))
        loudness = loudness * jnp.repeat(jnp.exp(heights), dims[axis_at] // blocks).reshape((-1,) + (1,) * (len(dims) - 1 - axis_at))
    return loudness


def noise(rng, dims, deviation, limit, shards=(), kind=jnp.bfloat16):
    values = deviation * jax.random.normal(rng, dims, jnp.float32)
    if shards:
        values = values * shard_levels(rng, dims, shards, -0.22, 0.18)
    return jnp.clip(values, -limit, limit).astype(kind)


def setup_inputs(seed: int = 0) -> dict:
    keys = jax.random.split(jax.random.key(seed), 8)
    video_qkv = draw_video_qkv(jax.random.fold_in(keys[7], 71), 0)
    audio_qkv = draw_audio_qkv(jax.random.fold_in(keys[7], 71), 0)
    head_slopes = jnp.clip(jnp.exp(math.log(0.8) - 2.7725887 * jax.random.uniform(keys[2], (HEADS,), jnp.float32) ** shard_levels(keys[2], (HEADS,), ((0, 16),), -0.2, 0.2)), 0.05, 0.8)
    audio_frame = draw_audio_frame(jax.random.fold_in(keys[7], 71), 0)
    out_weight = noise(keys[4], (HEADS * HEAD_DIM, D), (HEADS * HEAD_DIM) ** -0.5, 0.125, ((0, 16),))
    video_cot = noise(keys[5], (VIDEO, D), 1.0, 6.0, ((0, 16), (1, 16)))
    audio_cot = noise(keys[6], (AUDIO, HEADS * HEAD_DIM), 1.0, 6.0, ((0, 16), (1, 16)))
    return {"video_qkv": video_qkv, "audio_qkv": audio_qkv, "head_slopes": head_slopes, "audio_frame": audio_frame, "out_weight": out_weight, "video_cot": video_cot, "audio_cot": audio_cot}


def pair_scores(queries, key_part, query_frame, key_frame, slope_rate):
    scaling = HEAD_DIM ** -0.5
    scores = jnp.dot(queries, key_part.T, preferred_element_type=jnp.float32) * scaling
    if slope_rate is None:
        return scores
    return scores - slope_rate * jnp.abs(query_frame[:, None] - key_frame[None, :]).astype(jnp.float32)


def forward_rows(queries, query_frame, key_sets):
    scores = [pair_scores(queries, key_set[0], query_frame, key_set[2], key_set[3]) for key_set in key_sets]
    highest = jnp.maximum(jnp.max(scores[0], axis=1), jnp.max(scores[1], axis=1))
    summed = jnp.sum(jnp.exp(scores[0] - highest[:, None]), axis=1) + jnp.sum(jnp.exp(scores[1] - highest[:, None]), axis=1)
    log_norm = highest + jnp.log(summed)
    mixed_rows = jnp.dot(jnp.exp(scores[0] - log_norm[:, None]).astype(jnp.bfloat16), key_sets[0][1], preferred_element_type=jnp.float32)
    mixed_rows = mixed_rows + jnp.dot(jnp.exp(scores[1] - log_norm[:, None]).astype(jnp.bfloat16), key_sets[1][1], preferred_element_type=jnp.float32)
    return mixed_rows.astype(jnp.bfloat16), log_norm


def backward_rows(queries, query_frame, key_sets, grad_out, mixed_rows, log_norm):
    scaling = HEAD_DIM ** -0.5
    out_dot = jnp.sum(grad_out.astype(jnp.float32) * mixed_rows.astype(jnp.float32), axis=1)
    query_sum = jnp.zeros(queries.shape, jnp.float32)
    key_terms = []
    for key_part, value_part, key_frame, slope_rate in key_sets:
        scores = pair_scores(queries, key_part, query_frame, key_frame, slope_rate)
        probable = jnp.exp(scores - log_norm[:, None])
        prob_grad = jnp.dot(grad_out, value_part.T, preferred_element_type=jnp.float32)
        score_grad = (probable * (prob_grad - out_dot[:, None])).astype(jnp.bfloat16)
        query_sum = query_sum + jnp.dot(score_grad, key_part, preferred_element_type=jnp.float32)
        key_terms.append(jnp.dot(score_grad.T, queries, preferred_element_type=jnp.float32))
        key_terms.append(jnp.dot(probable.astype(jnp.bfloat16).T, grad_out, preferred_element_type=jnp.float32))
    return (query_sum * scaling).astype(jnp.bfloat16), key_terms


def reference(video_qkv, audio_qkv, head_slopes, audio_frame, out_weight, video_cot, audio_cot):
    scaling = HEAD_DIM ** -0.5
    video_frame = (jnp.arange(VIDEO) // FRAME_TOK).astype(jnp.int32)
    video_heads = video_qkv.reshape(3, VIDEO, HEADS, HEAD_DIM).transpose(2, 0, 1, 3)
    audio_heads = audio_qkv.reshape(3, AUDIO, HEADS, HEAD_DIM).transpose(2, 0, 1, 3)

    def key_sets(video_part, audio_part, slope_rate):
        video_side = ((video_part[1], video_part[2], video_frame, None), (audio_part[1], audio_part[2], audio_frame, slope_rate))
        audio_side = ((video_part[1], video_part[2], video_frame, slope_rate), (audio_part[1], audio_part[2], audio_frame, None))
        return video_side, audio_side

    def head_forward(head_item):
        video_part, audio_part, slope_rate = head_item
        video_side, audio_side = key_sets(video_part, audio_part, slope_rate)

        def video_block(block_item):
            return forward_rows(block_item[0], block_item[1], video_side)

        video_rows, video_norm = lax.map(video_block, (video_part[0].reshape(N_SEQ, TOK_DEV, HEAD_DIM), video_frame.reshape(N_SEQ, TOK_DEV)))
        audio_rows, audio_norm = forward_rows(audio_part[0], audio_frame, audio_side)
        return video_rows.reshape(VIDEO, HEAD_DIM), video_norm.reshape(VIDEO), audio_rows, audio_norm

    video_mix, video_norm, audio_mix, audio_norm = lax.map(head_forward, (video_heads, audio_heads, head_slopes))
    mixed_cols = video_mix.transpose(1, 0, 2).reshape(VIDEO, HEADS * HEAD_DIM)
    video_out = jnp.dot(mixed_cols, out_weight, preferred_element_type=jnp.float32).astype(jnp.bfloat16)
    grad_video = jnp.dot(video_cot, out_weight.T, preferred_element_type=jnp.float32).astype(jnp.bfloat16)
    grad_heads = grad_video.reshape(VIDEO, HEADS, HEAD_DIM).transpose(1, 0, 2)
    audio_grad_heads = audio_cot.reshape(AUDIO, HEADS, HEAD_DIM).transpose(1, 0, 2)

    def head_backward(head_item):
        video_part, audio_part, slope_rate, video_grads, audio_grads, video_rows, video_lognorm, audio_rows, audio_lognorm = head_item
        video_side, audio_side = key_sets(video_part, audio_part, slope_rate)

        def video_block(running, block_item):
            queries, frames, gradients, mixed_rows, lognorms = block_item
            query_grad, key_terms = backward_rows(queries, frames, video_side, gradients, mixed_rows, lognorms)
            return tuple(running[position] + key_terms[position] for position in range(4)), query_grad

        zero_video = jnp.zeros((VIDEO, HEAD_DIM), jnp.float32)
        zero_audio = jnp.zeros((AUDIO, HEAD_DIM), jnp.float32)
        blocks_in = (video_part[0].reshape(N_SEQ, TOK_DEV, HEAD_DIM), video_frame.reshape(N_SEQ, TOK_DEV),
                     video_grads.reshape(N_SEQ, TOK_DEV, HEAD_DIM), video_rows.reshape(N_SEQ, TOK_DEV, HEAD_DIM),
                     video_lognorm.reshape(N_SEQ, TOK_DEV))
        running, video_query = lax.scan(video_block, (zero_video, zero_video, zero_audio, zero_audio), blocks_in)
        audio_query, audio_terms = backward_rows(audio_part[0], audio_frame, audio_side, audio_grads, audio_rows, audio_lognorm)
        totals = [running[position] + audio_terms[position] for position in range(4)]
        video_stack = jnp.stack([video_query.reshape(VIDEO, HEAD_DIM), (totals[0] * scaling).astype(jnp.bfloat16), totals[1].astype(jnp.bfloat16)])
        audio_stack = jnp.stack([audio_query, (totals[2] * scaling).astype(jnp.bfloat16), totals[3].astype(jnp.bfloat16)])
        return video_stack, audio_stack

    video_grad, audio_grad = lax.map(head_backward, (video_heads, audio_heads, head_slopes, grad_heads, audio_grad_heads,
                                                     video_mix, video_norm, audio_mix, audio_norm))
    video_grad = video_grad.transpose(1, 2, 0, 3).reshape(3, VIDEO, HEADS * HEAD_DIM)
    audio_grad = audio_grad.transpose(1, 2, 0, 3).reshape(3, AUDIO, HEADS * HEAD_DIM)
    audio_out = audio_mix.transpose(1, 0, 2).reshape(AUDIO, HEADS * HEAD_DIM)
    return video_out, audio_out, video_grad, audio_grad
```

```python
import math

import jax
import jax.numpy as jnp
from jax import lax
from jax.experimental import pallas as pl
from jax.experimental.pallas import tpu as pltpu
from jax.sharding import PartitionSpec as P

BF = jnp.bfloat16
F32 = jnp.float32
HD = 128
TV = 128
TA = 64
TT = TV + TA
NY = 4
NX = 4
NZ = 8
QV = NX * TV
QA = NX * TA
QT = QV + QA
COLS = 192
HALF = NZ * COLS
LOG2E = 1.4426950408889634

NN = (((1,), (0,)), ((), ()))
NT = (((1,), (1,)), ((), ()))


def mm(a, b, dims=NN):
    return lax.dot_general(a, b, dims, preferred_element_type=F32)


def roll64(x):
    return pltpu.roll(x, 64, 1)


def low_half(rows):
    return lax.broadcasted_iota(jnp.int32, (rows, 128), 1) < 64


def kernel(
    vqkv, aqkv, slope_ref, frame_ref, w_hbm, cot_hbm, acot_hbm,
    out_ref, amix_ref, vgrad_ref, agrad_ref,
    kv, q, gb, cotb, cot_raw, w, wp, wsend, bias_v, bias_a, p_scr,
    osend, orecv, st_send, st_recv, col_scr, mix_own, mix_par,
    gp_send, gp_recv, g_send, dot_buf, os, orx,
    dkv_send, dkv_recv, dkv_own, dq_send, dq_recv,
    lsem, ssem, rsem,
):
    s = lax.axis_index("seq")
    grp = lax.axis_index("grp")
    y = lax.div(s, NX)
    xc = lax.rem(s, NX)
    x_lo = lax.div(grp, NZ)
    z = lax.rem(grp, NZ)
    core = lax.rem(xc, 2)
    sibling = (s + 1 - 2 * core, grp)
    cross = (s, lax.rem(grp + NZ, 2 * NZ))

    def y_peer(k):
        return (lax.rem(s + NX * k, NX * NY), grp)

    def x_slot(k):
        return lax.rem(xc + k, NX)

    def x_peer(k):
        return (y * NX + x_slot(k), grp)

    def z_slot(k):
        return lax.rem(z + k, NZ)

    def z_peer(k):
        return (s, x_lo * NZ + z_slot(k))

    sends = []
    count = [0]

    def remote(src, dst, to):
        i = count[0]
        count[0] += 1
        copy = pltpu.make_async_remote_copy(
            src_ref=src,
            dst_ref=dst,
            send_sem=ssem.at[i],
            recv_sem=rsem.at[i],
            device_id=to,
            device_id_type=pl.DeviceIdType.MESH,
        )
        copy.start()
        sends.append(copy)
        return copy

    local_count = [0]

    def local(src, dst):
        i = local_count[0]
        local_count[0] += 1
        copy = pltpu.make_async_copy(src, dst, lsem.at[i])
        copy.start()
        return copy

    barrier = pltpu.get_barrier_semaphore()
    peers = (
        [z_peer(k) for k in range(1, NZ)]
        + [cross]
        + [y_peer(k) for k in range(1, NY)]
        + [x_peer(k) for k in range(1, NX)]
    )
    for peer in peers:
        pl.semaphore_signal(barrier, inc=1, device_id=peer, device_id_type=pl.DeviceIdType.MESH)

    xv = pl.ds(pl.multiple_of(xc * TV, TV), TV)
    xa = pl.ds(pl.multiple_of(QV + xc * TA, TA), TA)
    l_cot = local(cot_hbm, cot_raw)
    l_w = local(w_hbm, w)
    l_kvv = local(vqkv.at[1:3], kv.at[:, y, 0:TV])
    l_kva = local(aqkv.at[1:3], kv.at[:, y, TV:TT])
    l_qv = local(vqkv.at[0], q.at[xv])
    l_qa = local(aqkv.at[0], q.at[xa])
    l_ga = local(acot_hbm, gb.at[xa])

    l_cot.wait()
    lane_r = lax.broadcasted_iota(jnp.int32, (64, 128), 0)
    lane_c = lax.broadcasted_iota(jnp.int32, (64, 128), 1)
    place_lo = (lane_r == lane_c).astype(BF)
    place_hi = (lane_r + 64 == lane_c).astype(BF)
    tail = cot_raw[:, 128:192]
    cotb[z, 0:128, :] = cot_raw[:, 0:128]
    cotb[z, 128:192, :] = (mm(tail[0:64], place_lo) + mm(tail[64:128], place_hi)).astype(BF)

    pl.semaphore_wait(barrier, len(peers))

    r_cot = [remote(cotb.at[z], cotb.at[z], z_peer(k)) for k in (4, 3, 5, 2, 6, 1, 7)]
    r_kv, r_q, r_ga = [], [], []
    for k in (2, 1, 3):
        r_kv.append(remote(vqkv.at[1:3], kv.at[:, y, 0:TV], y_peer(k)))
        r_kv.append(remote(aqkv.at[1:3], kv.at[:, y, TV:TT], y_peer(k)))
    for k in (2, 1, 3):
        r_q.append(remote(vqkv.at[0], q.at[xv], x_peer(k)))
        r_q.append(remote(aqkv.at[0], q.at[xa], x_peer(k)))

    def ordered(rows, base, store):
        count_rows = 64 if rows is not None else HD
        low = low_half(count_rows)

        def tile(n):
            cols = pl.ds(pl.multiple_of(base + 128 * n, 128), 128)
            return (w[rows, cols] if rows is not None else w[:, cols]).astype(F32)

        for p in range(NZ // 2):
            t1, t2 = tile(3 * p + 1), tile(3 * p + 2)
            store(2 * p, tile(3 * p))
            store(2 * p + 1, roll64(jnp.where(low, t2, t1)))
            store(NZ + p, jnp.where(low, t1, t2))

    l_w.wait()

    def store_send(n, value):
        wsend[:, 128 * n : 128 * (n + 1)] = value.astype(BF)

    def store_own(n, value):
        wp[0:HD, 128 * n : 128 * (n + 1)] = value.astype(BF)

    w_rows = pl.ds(pl.multiple_of(core * 64, 64), 64)
    wp_rows = pl.ds(pl.multiple_of(HD + core * 64, 64), 64)
    ordered(w_rows, (1 - x_lo) * HALF, store_send)
    r_w = remote(wsend, wp.at[wp_rows], cross)
    for k in (2, 1, 3):
        r_ga.append(remote(acot_hbm, gb.at[xa], x_peer(k)))
    ordered(None, x_lo * HALF, store_own)

    rate = slope_ref[0] * LOG2E
    key_lane = lax.broadcasted_iota(jnp.int32, (1, QV), 1)
    query_frame_v = (NY * 2 * y + lax.shift_right_logical(key_lane, 6)).astype(F32)
    two = pl.ds(2 * y, 2)
    query_frame_a = frame_ref[two, :].astype(F32)
    qfa = jnp.concatenate([query_frame_a[0:1], query_frame_a[1:2]], axis=1)
    row_v = lax.broadcasted_iota(jnp.int32, (TV, 1), 0)
    for slot in range(NY):
        frame_v = (8 * slot + 2 * xc + lax.shift_right_logical(row_v, 6)).astype(F32)
        bias_v[slot] = rate * jnp.abs(frame_v - qfa)
        one = frame_ref[pl.ds(2 * slot + lax.div(xc, 2), 1), :].astype(F32)
        turned = jnp.broadcast_to(one, (128, 128)).T
        frame_a = jnp.where(core == 1, turned[64:128], turned[0:64])[:, 0:1]
        bias_a[slot] = rate * jnp.abs(frame_a - query_frame_v)

    l_kvv.wait()
    l_kva.wait()
    l_qv.wait()
    l_qa.wait()
    for copy in r_kv + r_q:
        copy.wait_recv()
    c2 = HD ** (-0.5) * LOG2E
    keys = kv[0].reshape(NY * TT, HD)
    values_t = kv[1].reshape(NY * TT, HD).T
    for c in range(3):
        cols = slice(256 * c, 256 * (c + 1))
        scores = (mm(keys, q[cols, :], NT) * c2).reshape(NY, TT, 256)
        part_v, part_a = scores[:, 0:TV], scores[:, TV:TT]
        if c < 2:
            part_a = part_a - bias_a[:, :, cols]
        else:
            part_v = part_v - bias_v[...]
        high = jnp.maximum(
            jnp.max(part_v.reshape(NY * TV, 256), axis=0, keepdims=True),
            jnp.max(part_a.reshape(NY * TA, 256), axis=0, keepdims=True),
        )
        part_v = jnp.exp2(part_v - high)
        part_a = jnp.exp2(part_a - high)
        total = jnp.sum(part_v.reshape(NY * TV, 256), axis=0, keepdims=True) + jnp.sum(
            part_a.reshape(NY * TA, 256), axis=0, keepdims=True
        )
        p_scr[:, 0:TV, cols] = part_v
        p_scr[:, TV:TT, cols] = part_a
        probs = jnp.concatenate([part_v, part_a], axis=1).reshape(NY * TT, 256).astype(BF)
        mixed = mm(values_t, probs).T.astype(BF)
        if c < 2:
            osend[2 * c, 0:TV] = mixed[0:TV]
            osend[2 * c + 1, 0:TV] = mixed[TV:256]
        else:
            for owner in range(NX):
                osend[owner, TV:TT] = mixed[TA * owner : TA * (owner + 1)]
        st_send[0:1, cols] = high
        st_send[1:2, cols] = total
    r_st = [remote(st_send, st_recv.at[k - 1], x_peer(k)) for k in (2, 1, 3)]
    r_o = [remote(osend.at[x_slot(k)], orecv.at[k - 1], x_peer(k)) for k in (2, 1, 3)]

    r_w.wait_recv()
    r_w2 = remote(wp.at[wp_rows], wp.at[wp_rows], sibling)

    for copy in r_st:
        copy.wait_recv()
    highs = [st_send[0:1, :]] + [st_recv[k, 0:1, :] for k in range(3)]
    totals = [st_send[1:2, :]] + [st_recv[k, 1:2, :] for k in range(3)]
    top = jnp.maximum(jnp.maximum(highs[0], highs[1]), jnp.maximum(highs[2], highs[3]))
    scale = [jnp.exp2(h - top) for h in highs]
    norm = sum(t * e for t, e in zip(totals, scale))
    factor = [e / norm for e in scale]
    own_factor = factor[0]
    for k in range(4):
        col_scr[k : k + 1, :] = factor[k]

    turned_v = jnp.concatenate(
        [col_scr[:, xv]] + [jnp.zeros((120, 128), F32)], axis=0
    ).T
    audio_tile = pl.ds(pl.multiple_of(QV + lax.div(xc, 2) * 128, 128), 128)
    turned_a = jnp.concatenate(
        [col_scr[:, audio_tile]] + [jnp.zeros((120, 128), F32)], axis=0
    ).T
    turned_a = jnp.where(core == 1, turned_a[64:128], turned_a[0:64])
    for copy in r_o:
        copy.wait_recv()
    mine = osend[xc].astype(F32)
    mix_v = mine[0:TV] * turned_v[:, 0:1]
    mix_a = mine[TV:TT] * turned_a[:, 0:1]
    for k in range(3):
        other = orecv[k].astype(F32)
        mix_v = mix_v + other[0:TV] * turned_v[:, k + 1 : k + 2]
        mix_a = mix_a + other[TV:TT] * turned_a[:, k + 1 : k + 2]
    mix_vb = mix_v.astype(BF)
    mix_ab = mix_a.astype(BF)
    amix_ref[...] = mix_ab
    mix_own[...] = mix_vb
    r_mix = remote(mix_own, mix_par, cross)

    for copy in r_cot:
        copy.wait_recv()
    low = low_half(64)
    acc = jnp.zeros((TV, 256), F32)
    r_w2.wait_recv()
    for p in range(NZ // 2):
        even, odd = cotb[2 * p], cotb[2 * p + 1]
        lead = jnp.concatenate([even[0:128], odd[0:128]], axis=1)
        acc = acc + mm(lead, wp[:, 256 * p : 256 * (p + 1)], NT)
        be, bo = even[128:192].astype(F32), odd[128:192].astype(F32)
        tails = jnp.concatenate(
            [jnp.where(low, be, roll64(bo)), jnp.where(low, roll64(be), bo)], axis=0
        ).astype(BF)
        acc = acc + mm(tails, wp[:, 1024 + 128 * p : 1024 + 128 * (p + 1)], NT)
    gp_send[...] = acc[:, 128:256].astype(BF)
    r_gp = remote(gp_send, gp_recv, cross)
    l_ga.wait()
    dot_a = jnp.sum(
        jnp.concatenate([gb[xa, :].astype(F32) * mix_ab.astype(F32), jnp.zeros((64, 128), F32)], axis=0).T,
        axis=0,
        keepdims=True,
    )
    r_gp.wait_recv()
    grad = (acc[:, 0:128] + gp_recv[...].astype(F32)).astype(BF)
    g_send[...] = grad
    gb[xv, :] = grad
    r_g = [remote(g_send, gb.at[xv], x_peer(k)) for k in (2, 1, 3)]
    dot_v = jnp.sum((grad.astype(F32) * mix_vb.astype(F32)).T, axis=0, keepdims=True)
    dot_buf[xc, 0:1, 0:128] = dot_v
    dot_buf[xc, 0:1, 128:256] = dot_a
    r_dot = [remote(dot_buf.at[xc], dot_buf.at[xc], x_peer(k)) for k in (2, 1, 3)]

    r_mix.wait_recv()
    both = jnp.concatenate([mix_own[...], mix_par[...]], axis=1)
    for p in range(NZ // 2):
        lead = mm(both, wp[:, 256 * p : 256 * (p + 1)])
        tails = mm(both, wp[:, 1024 + 128 * p : 1024 + 128 * (p + 1)])
        os[2 * p, 0:128] = lead[:, 0:128].astype(BF)
        os[2 * p + 1, 0:128] = lead[:, 128:256].astype(BF)
        upper, lower = tails[0:64], tails[64:128]
        os[2 * p, 128:192] = jnp.where(low, upper, roll64(lower)).astype(BF)
        os[2 * p + 1, 128:192] = jnp.where(low, roll64(upper), lower).astype(BF)
    r_os = [remote(os.at[z_slot(k)], orx.at[k - 1], z_peer(k)) for k in (4, 3, 5, 2, 6, 1, 7)]

    for copy in r_ga + r_g + r_dot:
        copy.wait_recv()
    dots = [dot_buf[k, 0:1, :] for k in range(NX)]
    one_low = low_half(1)
    dot = jnp.concatenate(
        [d[:, 0:128] for d in dots]
        + [
            jnp.where(one_low, dots[0][:, 128:256], roll64(dots[1][:, 128:256])),
            jnp.where(one_low, dots[2][:, 128:256], roll64(dots[3][:, 128:256])),
        ],
        axis=1,
    )
    c = HD ** (-0.5)
    dq_t = jnp.zeros((HD, QT), F32)
    r_dkv = []
    for k in (2, 1, 3, 0):
        slot = lax.rem(y + k, NY)
        key, value = kv[0, slot], kv[1, slot]
        prob = p_scr[slot] * own_factor
        dp = mm(value, gb[...], NT)
        ds = (prob * (dp - dot)).astype(BF)
        dv = mm(prob.astype(BF), gb[...])
        dk = mm(ds, q[...]) * c
        if k:
            dkv_send[k - 1, 0] = dk.astype(BF)
            dkv_send[k - 1, 1] = dv.astype(BF)
            r_dkv.append(remote(dkv_send.at[k - 1], dkv_recv.at[k - 1], y_peer(k)))
        else:
            dkv_own[0] = dk
            dkv_own[1] = dv
        dq_t = dq_t + mm(key.T, ds)
    dq = (dq_t * c).T.astype(BF)
    for owner in range(NX):
        dq_send[owner, 0:TV] = dq[TV * owner : TV * (owner + 1)]
        dq_send[owner, TV:TT] = dq[QV + TA * owner : QV + TA * (owner + 1)]
    r_dq = [remote(dq_send.at[x_slot(k)], dq_recv.at[k - 1], x_peer(k)) for k in (2, 1, 3)]

    for copy in r_os:
        copy.wait_recv()
    total = os[z].astype(F32)
    for k in range(NZ - 1):
        total = total + orx[k].astype(F32)
    out_ref[:, 0:128] = total[0:128].astype(BF)
    packed = total[128:192]
    out_ref[0:64, 128:192] = packed[:, 0:64].astype(BF)
    out_ref[64:128, 128:192] = roll64(packed)[:, 0:64].astype(BF)
    for copy in r_dkv:
        copy.wait_recv()
    dkv = dkv_own[...]
    for k in range(3):
        dkv = dkv + dkv_recv[k].astype(F32)
    dkv = dkv.astype(BF)
    vgrad_ref[1:3] = dkv[:, 0:TV]
    agrad_ref[1:3] = dkv[:, TV:TT]
    for copy in r_dq:
        copy.wait_recv()
    dq = dq_send[xc].astype(F32)
    for k in range(3):
        dq = dq + dq_recv[k].astype(F32)
    dq = dq.astype(BF)
    vgrad_ref[0] = dq[0:TV]
    agrad_ref[0] = dq[TV:TT]
    for copy in sends:
        copy.wait_send()


def per_device(video_qkv, audio_qkv, head_slopes, audio_frame, out_weight, video_cot, audio_cot):
    any_spec = pl.BlockSpec(memory_space=pl.ANY)
    vmem = pl.BlockSpec(memory_space=pltpu.VMEM)
    smem = pl.BlockSpec(memory_space=pltpu.SMEM)
    scratch = [
        pltpu.VMEM((2, NY, TT, HD), BF),
        pltpu.VMEM((QT, HD), BF),
        pltpu.VMEM((QT, HD), BF),
        pltpu.VMEM((NZ, 192, 128), BF),
        pltpu.VMEM((TV, COLS), BF),
        pltpu.VMEM((HD, 2 * HALF), BF),
        pltpu.VMEM((2 * HD, HALF), BF),
        pltpu.VMEM((64, HALF), BF),
        pltpu.VMEM((NY, TV, QA), F32),
        pltpu.VMEM((NY, TA, QV), F32),
        pltpu.VMEM((NY, TT, QT), F32),
        pltpu.VMEM((NX, TT, HD), BF),
        pltpu.VMEM((3, TT, HD), BF),
        pltpu.VMEM((8, QT), F32),
        pltpu.VMEM((3, 8, QT), F32),
        pltpu.VMEM((8, QT), F32),
        pltpu.VMEM((TV, HD), BF),
        pltpu.VMEM((TV, HD), BF),
        pltpu.VMEM((TV, HD), BF),
        pltpu.VMEM((TV, HD), BF),
        pltpu.VMEM((TV, HD), BF),
        pltpu.VMEM((NX, 8, 256), F32),
        pltpu.VMEM((NZ, 192, 128), BF),
        pltpu.VMEM((NZ - 1, 192, 128), BF),
        pltpu.VMEM((3, 2, TT, HD), BF),
        pltpu.VMEM((3, 2, TT, HD), BF),
        pltpu.VMEM((2, TT, HD), F32),
        pltpu.VMEM((NX, TT, HD), BF),
        pltpu.VMEM((3, TT, HD), BF),
        pltpu.SemaphoreType.DMA((8,)),
        pltpu.SemaphoreType.DMA((64,)),
        pltpu.SemaphoreType.DMA((64,)),
    ]
    return pl.pallas_call(
        kernel,
        out_shape=(
            jax.ShapeDtypeStruct((TV, COLS), BF),
            jax.ShapeDtypeStruct((TA, HD), BF),
            jax.ShapeDtypeStruct((3, TV, HD), BF),
            jax.ShapeDtypeStruct((3, TA, HD), BF),
        ),
        in_specs=[any_spec, any_spec, smem, vmem, any_spec, any_spec, any_spec],
        out_specs=(vmem, vmem, vmem, vmem),
        scratch_shapes=scratch,
        compiler_params=pltpu.CompilerParams(
            collective_id=0, has_side_effects=True, vmem_limit_bytes=56 * 1024 * 1024
        ),
    )(
        video_qkv,
        audio_qkv,
        head_slopes,
        audio_frame.reshape(8, 128),
        out_weight,
        video_cot,
        audio_cot,
    )


def solution(mesh):
    in_specs = (
        P(None, "seq", "grp"),
        P(None, "seq", "grp"),
        P("grp"),
        P(),
        P("grp", None),
        P("seq", "grp"),
        P("seq", "grp"),
    )
    out_specs = (P("seq", "grp"), P("seq", "grp"), P(None, "seq", "grp"), P(None, "seq", "grp"))
    return jax.shard_map(
        per_device, mesh=mesh, in_specs=in_specs, out_specs=out_specs, check_vma=False
    )
```

```python
import math

import jax
import jax.numpy as jnp
from jax import lax
from jax.experimental import pallas as pl
from jax.experimental.pallas import tpu as pltpu
from jax.sharding import PartitionSpec as P

BF = jnp.bfloat16
F32 = jnp.float32
HD = 128
TV = 128
TA = 64
TT = TV + TA
NY = 4
NS = 2 * NY
NZ = 8
QV = 2 * TV
QA = 2 * TA
QT = QV + QA
COLS = 192
HALF = NZ * COLS
LOG2E = 1.4426950408889634
AT_V = COLS + TA
AT_A = AT_V + 3 * TV

NN = (((1,), (0,)), ((), ()))
NT = (((1,), (1,)), ((), ()))


def mm(a, b, dims=NN):
    return lax.dot_general(a, b, dims, preferred_element_type=F32)


def roll64(x):
    return pltpu.roll(x, 64, 1)


def low_half(rows):
    return lax.broadcasted_iota(jnp.int32, (rows, 128), 1) < 64


def kernel(
    vqkv, aqkv, slope_ref, frame_ref, w_hbm, cot_hbm, acot_hbm,
    res_ref,
    kv, q, gb, cotb, wp, wpt, bias_v, bias_a, p_scr,
    osend, orecv, st_send, st_recv, col_scr, mix_own, mix_par,
    gp_send, gp_recv, g_send, dot_buf, os, orx, ofar, ofar_recv,
    sib_send, sib_recv, dkv_send, dkv_recv, dkv_own, dq_send, dq_recv,
    lsem, ssem, rsem,
):
    s = lax.axis_index("seq")
    grp = lax.axis_index("grp")
    y = lax.div(s, 4)
    x_hi = lax.div(lax.rem(s, 4), 2)
    core = lax.rem(s, 2)
    x_lo = lax.div(grp, NZ)
    z = lax.rem(grp, NZ)
    sibling = (s + 1 - 2 * core, grp)
    partner = (s + 2 - 4 * x_hi, grp)
    cross = (s, lax.rem(grp + NZ, 2 * NZ))

    def y_slot(k):
        return lax.rem(y + k, NY)

    def y_peer(k):
        return (lax.rem(s + 4 * k, 4 * NY), grp)

    def z_slot(k):
        return lax.rem(z + k, NZ)

    def z_peer(k):
        return (s, x_lo * NZ + z_slot(k))

    sends = []
    count = [0]

    def remote(src, dst, to):
        i = count[0]
        count[0] += 1
        copy = pltpu.make_async_remote_copy(
            src_ref=src,
            dst_ref=dst,
            send_sem=ssem.at[i],
            recv_sem=rsem.at[i],
            device_id=to,
            device_id_type=pl.DeviceIdType.MESH,
        )
        copy.start()
        sends.append(copy)
        return copy

    local_count = [0]

    def local(src, dst):
        i = local_count[0]
        local_count[0] += 1
        copy = pltpu.make_async_copy(src, dst, lsem.at[i])
        copy.start()
        return copy

    barrier = pltpu.get_barrier_semaphore()
    peers = (
        [z_peer(k) for k in range(1, NZ)]
        + [cross, sibling, partner]
        + [y_peer(k) for k in range(1, NY)]
    )
    for peer in peers:
        pl.semaphore_signal(barrier, inc=1, device_id=peer, device_id_type=pl.DeviceIdType.MESH)

    xv = pl.ds(pl.multiple_of(x_hi * TV, TV), TV)
    xa = pl.ds(pl.multiple_of(QV + x_hi * TA, TA), TA)
    zr = pl.ds(pl.multiple_of(z * COLS, 64), COLS)
    own_cols = pl.ds(pl.multiple_of(x_lo * HALF, HALF), HALF)
    other_cols = pl.ds(pl.multiple_of((1 - x_lo) * HALF, HALF), HALF)
    slot_own = NY * core + y
    l_cot = local(cot_hbm, cotb.at[zr])
    l_w = local(w_hbm.at[:, own_cols], wp.at[0:HD])
    l_kvv = local(vqkv.at[1:3], kv.at[:, slot_own, 0:TV])
    l_kva = local(aqkv.at[1:3], kv.at[:, slot_own, TV:TT])
    l_qv = local(vqkv.at[0], q.at[xv])
    l_qa = local(aqkv.at[0], q.at[xa])
    l_ga = local(acot_hbm, gb.at[xa])

    pl.semaphore_wait(barrier, len(peers))

    def send_kv(to):
        return [
            remote(vqkv.at[1:3], kv.at[:, slot_own, 0:TV], to),
            remote(aqkv.at[1:3], kv.at[:, slot_own, TV:TT], to),
        ]

    r_cot = {k: remote(cot_hbm, cotb.at[zr], z_peer(k)) for k in (2, 6)}
    r_kv = {k: send_kv(y_peer(k)) for k in (1, 3, 2)}
    w_rows = pl.ds(pl.multiple_of(core * 64, 64), 64)
    wp_rows = pl.ds(pl.multiple_of(HD + core * 64, 64), 64)
    r_w = remote(w_hbm.at[w_rows, other_cols], wp.at[wp_rows], cross)
    r_q = [remote(vqkv.at[0], q.at[xv], partner), remote(aqkv.at[0], q.at[xa], partner)]
    for k in (3, 5, 1, 7):
        r_cot[k] = remote(cot_hbm, cotb.at[zr], z_peer(k))
    r_sib = send_kv(sibling)
    r_ga = remote(acot_hbm, gb.at[xa], partner)

    rate = slope_ref[0] * LOG2E
    low1 = low_half(1)
    lane = lax.broadcasted_iota(jnp.int32, (1, QV), 1)
    lane_slot = lax.shift_right_logical(lane, 7)
    lane_frame = lax.shift_right_logical(lane, 6) - 2 * lane_slot
    query_frame_v = (8 * y + 4 * lane_slot + 2 * core + lane_frame).astype(F32)
    first = frame_ref[pl.ds(2 * y, 1), :].astype(F32)
    second = frame_ref[pl.ds(2 * y + 1, 1), :].astype(F32)
    query_frame_a = jnp.where(
        core == 0,
        jnp.where(low1, first, roll64(second)),
        jnp.where(low1, roll64(first), second),
    )
    row_frame = lax.shift_right_logical(lax.broadcasted_iota(jnp.int32, (TV, 1), 0), 6)
    for slot in range(NY):
        one = frame_ref[pl.ds(2 * slot + x_hi, 1), :].astype(F32)
        turned = jnp.broadcast_to(one, (128, 128)).T
        for c in range(2):
            frame_v = (8 * slot + 4 * x_hi + 2 * c + row_frame).astype(F32)
            bias_v[NY * c + slot] = rate * jnp.abs(frame_v - query_frame_a)
            frame_a = turned[64 * c : 64 * (c + 1), 0:1]
            bias_a[NY * c + slot] = rate * jnp.abs(frame_a - query_frame_v)

    for k in (1, 3):
        for copy in r_kv[k]:
            copy.wait_recv()
        at = NY * core + y_slot(NY - k)
        r_sib.append(remote(kv.at[:, at], kv.at[:, at], sibling))
    r_far = []
    for k, half in ((2, 0), (6, 1)):
        r_cot[k].wait_recv()
        rows = pl.ds(pl.multiple_of(z_slot(NZ - k) * COLS + half * 96, 32), 96)
        r_far.append(remote(cotb.at[rows], cotb.at[rows], z_peer(k)))
    l_w.wait()
    wpt[:, 0:HD] = wp[0:HD, :].T
    r_w.wait_recv()
    r_w2 = remote(wp.at[wp_rows], wp.at[wp_rows], sibling)
    for copy in r_kv[2]:
        copy.wait_recv()
    at = NY * core + y_slot(2)
    r_sib.append(remote(kv.at[:, at], kv.at[:, at], sibling))

    l_cot.wait()
    for k in (3, 5, 1, 7):
        r_cot[k].wait_recv()
    for copy in r_far:
        copy.wait_recv()
    r_w2.wait_recv()
    cot_all = cotb[...]
    gp_send[...] = mm(wp[HD : 2 * HD, :], cot_all).astype(BF)
    r_gp = remote(gp_send, gp_recv, cross)
    grad_own = mm(wp[0:HD, :], cot_all)

    l_kvv.wait()
    l_kva.wait()
    l_qv.wait()
    l_qa.wait()
    for copy in r_q + r_sib:
        copy.wait_recv()
    c2 = HD ** (-0.5) * LOG2E
    keys = kv[0].reshape(NS * TT, HD)
    values_t = kv[1].reshape(NS * TT, HD).T
    for c, cols in enumerate((slice(0, QV), slice(QV, QT))):
        wide = cols.stop - cols.start
        scores = (mm(keys, q[cols, :], NT) * c2).reshape(NS, TT, wide)
        part_v, part_a = scores[:, 0:TV], scores[:, TV:TT]
        if c == 0:
            part_a = part_a - bias_a[...]
        else:
            part_v = part_v - bias_v[...]
        high = jnp.maximum(
            jnp.max(part_v.reshape(NS * TV, wide), axis=0, keepdims=True),
            jnp.max(part_a.reshape(NS * TA, wide), axis=0, keepdims=True),
        )
        part_v = jnp.exp2(part_v - high)
        part_a = jnp.exp2(part_a - high)
        total = jnp.sum(part_v.reshape(NS * TV, wide), axis=0, keepdims=True) + jnp.sum(
            part_a.reshape(NS * TA, wide), axis=0, keepdims=True
        )
        p_scr[:, 0:TV, cols] = part_v
        p_scr[:, TV:TT, cols] = part_a
        probs = jnp.concatenate([part_v, part_a], axis=1).reshape(NS * TT, wide).astype(BF)
        mixed = mm(values_t, probs).T.astype(BF)
        rows_each = wide // 2
        for owner in range(2):
            piece = mixed[rows_each * owner : rows_each * (owner + 1)]
            if c == 0:
                osend[owner, 0:TV] = piece
            else:
                osend[owner, TV:TT] = piece
        st_send[0:1, cols] = high
        st_send[1:2, cols] = total
    r_st = remote(st_send, st_recv, partner)
    r_o = remote(osend.at[1 - x_hi], orecv, partner)

    r_gp.wait_recv()
    grad_t = (grad_own + gp_recv[...].astype(F32)).astype(BF).astype(F32)
    grad = grad_t.T.astype(BF)
    g_send[...] = grad
    gb[xv, :] = grad
    r_g = remote(g_send, gb.at[xv], partner)
    wpt[:, HD : 2 * HD] = wp[HD : 2 * HD, :].T

    r_st.wait_recv()
    top = jnp.maximum(st_send[0:1, :], st_recv[0:1, :])
    e_own = jnp.exp2(st_send[0:1, :] - top)
    e_other = jnp.exp2(st_recv[0:1, :] - top)
    norm = st_send[1:2, :] * e_own + st_recv[1:2, :] * e_other
    own_factor = e_own / norm
    col_scr[0:1, :] = own_factor
    col_scr[1:2, :] = e_other / norm

    pad = jnp.zeros((120, 128), F32)
    turned_v = jnp.concatenate([col_scr[:, xv], pad], axis=0).T
    turned_a = jnp.concatenate([col_scr[:, QV:QT], pad], axis=0).T
    turned_a = jnp.where(x_hi == 1, turned_a[64:128], turned_a[0:64])
    r_o.wait_recv()
    mine, other = osend[x_hi].astype(F32), orecv[...].astype(F32)
    mix_v = mine[0:TV] * turned_v[:, 0:1] + other[0:TV] * turned_v[:, 1:2]
    mix_a = mine[TV:TT] * turned_a[:, 0:1] + other[TV:TT] * turned_a[:, 1:2]
    mix_vb = mix_v.astype(BF)
    mix_ab = mix_a.astype(BF)
    mix_own[...] = mix_vb
    r_mix = remote(mix_own, mix_par, cross)
    res_ref[COLS : COLS + TA, :] = mix_ab
    l_ga.wait()
    dot_a = jnp.sum(
        jnp.concatenate(
            [gb[xa, :].astype(F32) * mix_ab.astype(F32), jnp.zeros((64, 128), F32)], axis=0
        ).T,
        axis=0,
        keepdims=True,
    )
    dot_v = jnp.sum(grad_t * mix_vb.astype(F32).T, axis=0, keepdims=True)
    dot_buf[x_hi, 0:1, 0:128] = dot_v
    dot_buf[x_hi, 0:1, 128:256] = dot_a
    r_dot = remote(dot_buf.at[x_hi], dot_buf.at[x_hi], partner)

    r_mix.wait_recv()
    both = jnp.concatenate([mix_own[...], mix_par[...]], axis=1)
    os[...] = mm(wpt[...], both, NT).astype(BF).reshape(NZ, COLS, HD)
    r_ofar = [
        remote(os.at[z_slot(4), 96 * half : 96 * (half + 1)], ofar_recv.at[half], z_peer(k))
        for k, half in ((2, 0), (6, 1))
    ]
    r_os = {k: remote(os.at[z_slot(k)], orx.at[k - 1], z_peer(k)) for k in (3, 5, 1, 7)}

    for copy in (r_ga, r_g, r_dot):
        copy.wait_recv()
    dots = [dot_buf[k, 0:1, :] for k in range(2)]
    dot = jnp.concatenate(
        [dots[0][:, 0:128], dots[1][:, 0:128]]
        + [jnp.where(low1, dots[0][:, 128:256], roll64(dots[1][:, 128:256]))],
        axis=1,
    )
    c = HD ** (-0.5)
    dq_t = jnp.zeros((HD, QT), F32)
    r_half, r_dkv = {}, []
    for mine, k in (
        (0, 2), (0, 1), (1, 2), (0, 3), (1, 1), (0, 0), (1, 3), (1, 0),
    ):
        slot = NY * (core if mine else 1 - core) + y_slot(k)
        key, value = kv[0, slot], kv[1, slot]
        prob = p_scr[slot] * own_factor
        dp = mm(value, gb[...], NT)
        ds = (prob * (dp - dot)).astype(BF)
        dv = mm(prob.astype(BF), gb[...])
        dk = mm(ds, q[...]) * c
        dq_t = dq_t + mm(key.T, ds)
        if not mine:
            sib_send[k, 0] = dk.astype(BF)
            sib_send[k, 1] = dv.astype(BF)
            r_half[k] = remote(sib_send.at[k], sib_recv.at[k], sibling)
        elif k:
            r_half[k].wait_recv()
            dkv_send[k - 1, 0] = (dk + sib_recv[k, 0].astype(F32)).astype(BF)
            dkv_send[k - 1, 1] = (dv + sib_recv[k, 1].astype(F32)).astype(BF)
            r_dkv.append(remote(dkv_send.at[k - 1], dkv_recv.at[k - 1], y_peer(k)))
        else:
            dkv_own[0] = dk
            dkv_own[1] = dv
        if (mine, k) == (1, 2):
            for at, half in ((2, 0), (6, 1)):
                r_ofar[half].wait_recv()
                rows = slice(96 * half, 96 * (half + 1))
                share = os[z_slot(at), rows].astype(F32) + ofar_recv[half].astype(F32)
                ofar[half, rows] = share.astype(BF)
                rest = slice(96 * (1 - half), 96 * (2 - half))
                ofar[half, rest] = os[z_slot(at), rest]
                r_os[at] = remote(ofar.at[half], orx.at[at - 1], z_peer(at))
    dq = (dq_t * c).T.astype(BF)
    for owner in range(2):
        dq_send[owner, 0:TV] = dq[TV * owner : TV * (owner + 1)]
        dq_send[owner, TV:TT] = dq[QV + TA * owner : QV + TA * (owner + 1)]
    r_dq = remote(dq_send.at[1 - x_hi], dq_recv, partner)

    total = os[z].astype(F32)
    for k in (3, 5, 1, 7, 2, 6):
        r_os[k].wait_recv()
        total = total + orx[k - 1].astype(F32)
    res_ref[0:COLS, :] = total.astype(BF)
    r_half[0].wait_recv()
    dkv = dkv_own[...] + sib_recv[0].astype(F32)
    for copy in r_dkv:
        copy.wait_recv()
    for k in range(3):
        dkv = dkv + dkv_recv[k].astype(F32)
    dkv = dkv.astype(BF)
    for n in range(2):
        res_ref[AT_V + TV * (n + 1) : AT_V + TV * (n + 2), :] = dkv[n, 0:TV]
        res_ref[AT_A + TA * (n + 1) : AT_A + TA * (n + 2), :] = dkv[n, TV:TT]
    r_dq.wait_recv()
    dq = (dq_send[x_hi].astype(F32) + dq_recv[...].astype(F32)).astype(BF)
    res_ref[AT_V : AT_V + TV, :] = dq[0:TV]
    res_ref[AT_A : AT_A + TA, :] = dq[TV:TT]
    for copy in sends:
        copy.wait_send()


def unpack(res, out_ref, amix_ref, vgrad_ref, agrad_ref):
    out_ref[...] = res[0:COLS, :]
    amix_ref[...] = res[COLS : COLS + TA, :]
    vgrad_ref[...] = res[AT_V:AT_A, :].reshape(3, TV, HD)
    agrad_ref[...] = res[AT_A : AT_A + 3 * TA, :].reshape(3, TA, HD)


def per_device(video_qkv, audio_qkv, head_slopes, audio_frame, out_weight, video_cot, audio_cot):
    any_spec = pl.BlockSpec(memory_space=pl.ANY)
    vmem = pl.BlockSpec(memory_space=pltpu.VMEM)
    smem = pl.BlockSpec(memory_space=pltpu.SMEM)
    scratch = [
        pltpu.VMEM((2, NS, TT, HD), BF),
        pltpu.VMEM((QT, HD), BF),
        pltpu.VMEM((QT, HD), BF),
        pltpu.VMEM((HALF, TV), BF),
        pltpu.VMEM((2 * HD, HALF), BF),
        pltpu.VMEM((HALF, 2 * HD), BF),
        pltpu.VMEM((NS, TV, QA), F32),
        pltpu.VMEM((NS, TA, QV), F32),
        pltpu.VMEM((NS, TT, QT), F32),
        pltpu.VMEM((2, TT, HD), BF),
        pltpu.VMEM((TT, HD), BF),
        pltpu.VMEM((8, QT), F32),
        pltpu.VMEM((8, QT), F32),
        pltpu.VMEM((8, QT), F32),
        pltpu.VMEM((TV, HD), BF),
        pltpu.VMEM((TV, HD), BF),
        pltpu.VMEM((TV, HD), BF),
        pltpu.VMEM((TV, HD), BF),
        pltpu.VMEM((TV, HD), BF),
        pltpu.VMEM((2, 8, 256), F32),
        pltpu.VMEM((NZ, COLS, HD), BF),
        pltpu.VMEM((NZ - 1, COLS, HD), BF),
        pltpu.VMEM((2, COLS, HD), BF),
        pltpu.VMEM((2, COLS // 2, HD), BF),
        pltpu.VMEM((NY, 2, TT, HD), BF),
        pltpu.VMEM((NY, 2, TT, HD), BF),
        pltpu.VMEM((3, 2, TT, HD), BF),
        pltpu.VMEM((3, 2, TT, HD), BF),
        pltpu.VMEM((2, TT, HD), F32),
        pltpu.VMEM((2, TT, HD), BF),
        pltpu.VMEM((TT, HD), BF),
        pltpu.SemaphoreType.DMA((8,)),
        pltpu.SemaphoreType.DMA((48,)),
        pltpu.SemaphoreType.DMA((48,)),
    ]
    res = pl.pallas_call(
        kernel,
        out_shape=jax.ShapeDtypeStruct((AT_A + 3 * TA, HD), BF),
        in_specs=[any_spec, any_spec, smem, vmem, any_spec, any_spec, any_spec],
        out_specs=vmem,
        scratch_shapes=scratch,
        compiler_params=pltpu.CompilerParams(
            collective_id=0, has_side_effects=True, vmem_limit_bytes=56 * 1024 * 1024
        ),
    )(
        video_qkv,
        audio_qkv,
        head_slopes,
        audio_frame.reshape(8, 128),
        out_weight,
        video_cot.T,
        audio_cot,
    )
    out_t, audio_mix, video_grad, audio_grad = pl.pallas_call(
        unpack,
        out_shape=(
            jax.ShapeDtypeStruct((COLS, TV), BF),
            jax.ShapeDtypeStruct((TA, HD), BF),
            jax.ShapeDtypeStruct((3, TV, HD), BF),
            jax.ShapeDtypeStruct((3, TA, HD), BF),
        ),
        in_specs=[vmem],
        out_specs=(vmem,) * 4,
    )(res)
    return out_t.T, audio_mix, video_grad, audio_grad


def solution(mesh):
    in_specs = (
        P(None, "seq", "grp"),
        P(None, "seq", "grp"),
        P("grp"),
        P(),
        P("grp", None),
        P("seq", "grp"),
        P("seq", "grp"),
    )
    out_specs = (P("seq", "grp"), P("seq", "grp"), P(None, "seq", "grp"), P(None, "seq", "grp"))
    return jax.shard_map(
        per_device, mesh=mesh, in_specs=in_specs, out_specs=out_specs, check_vma=False
    )
```

```python
import math

import jax
import jax.numpy as jnp
from jax import lax
from jax.experimental import pallas as pl
from jax.experimental.pallas import tpu as pltpu
from jax.sharding import PartitionSpec as P

BF = jnp.bfloat16
F32 = jnp.float32
HD = 128
TV = 128
TA = 64
TT = TV + TA
NY = 4
NS = 2 * NY
NZ = 8
QV = 2 * TV
QA = 2 * TA
QT = QV + QA
COLS = 192
HALF = NZ * COLS
LOG2E = 1.4426950408889634
AT_V = COLS + TA
AT_A = AT_V + 3 * TV

NN = (((1,), (0,)), ((), ()))
NT = (((1,), (1,)), ((), ()))


def mm(a, b, dims=NN):
    return lax.dot_general(a, b, dims, preferred_element_type=F32)


def roll64(x):
    return pltpu.roll(x, 64, 1)


def low_half(rows):
    return lax.broadcasted_iota(jnp.int32, (rows, 128), 1) < 64


def kernel(
    vqkv, aqkv, slope_ref, frame_ref, w_hbm, cot_hbm, acot_hbm,
    res_ref,
    kv, q, gb, cotb, wp, wpt, bias_v, bias_a, p_scr,
    osend, orecv, oc_recv, od_recv, st_send, st_recv, col_scr,
    gp_send, gp_recv, go_send, go_recv, gd_recv, dot_buf, os, orx, ofar, ofar_recv,
    sib_send, sib_recv, dkv_send, dkv_recv, dkv_own, dq_send, dq_recv,
    lsem, ssem, rsem,
):
    s = lax.axis_index("seq")
    grp = lax.axis_index("grp")
    y = lax.div(s, 4)
    x_hi = lax.div(lax.rem(s, 4), 2)
    core = lax.rem(s, 2)
    x_lo = lax.div(grp, NZ)
    z = lax.rem(grp, NZ)
    sibling = (s + 1 - 2 * core, grp)
    partner = (s + 2 - 4 * x_hi, grp)
    cross = (s, lax.rem(grp + NZ, 2 * NZ))
    corner = (s + 2 - 4 * x_hi, lax.rem(grp + NZ, 2 * NZ))

    def y_slot(k):
        return lax.rem(y + k, NY)

    def y_peer(k):
        return (lax.rem(s + 4 * k, 4 * NY), grp)

    def z_slot(k):
        return lax.rem(z + k, NZ)

    def z_peer(k):
        return (s, x_lo * NZ + z_slot(k))

    sends = []
    count = [0]

    def remote(src, dst, to):
        i = count[0]
        count[0] += 1
        copy = pltpu.make_async_remote_copy(
            src_ref=src,
            dst_ref=dst,
            send_sem=ssem.at[i],
            recv_sem=rsem.at[i],
            device_id=to,
            device_id_type=pl.DeviceIdType.MESH,
        )
        copy.start()
        sends.append(copy)
        return copy

    local_count = [0]

    def local(src, dst):
        i = local_count[0]
        local_count[0] += 1
        copy = pltpu.make_async_copy(src, dst, lsem.at[i])
        copy.start()
        return copy

    barrier = pltpu.get_barrier_semaphore()
    peers = (
        [z_peer(k) for k in range(1, NZ)]
        + [cross, corner, sibling, partner]
        + [y_peer(k) for k in range(1, NY)]
    )
    for peer in peers:
        pl.semaphore_signal(barrier, inc=1, device_id=peer, device_id_type=pl.DeviceIdType.MESH)

    xv = pl.ds(pl.multiple_of(x_hi * TV, TV), TV)
    xa = pl.ds(pl.multiple_of(QV + x_hi * TA, TA), TA)
    zr = pl.ds(pl.multiple_of(z * COLS, 64), COLS)
    own_cols = pl.ds(pl.multiple_of(x_lo * HALF, HALF), HALF)
    other_cols = pl.ds(pl.multiple_of((1 - x_lo) * HALF, HALF), HALF)
    slot_own = NY * core + y
    l_cot = local(cot_hbm, cotb.at[zr])
    l_w = local(w_hbm.at[:, own_cols], wp.at[0:HD])
    l_kvv = local(vqkv.at[1:3], kv.at[:, slot_own, 0:TV])
    l_kva = local(aqkv.at[1:3], kv.at[:, slot_own, TV:TT])
    l_qv = local(vqkv.at[0], q.at[xv])
    l_qa = local(aqkv.at[0], q.at[xa])
    l_ga = local(acot_hbm, gb.at[xa])

    pl.semaphore_wait(barrier, len(peers))

    def send_kv(to):
        return [
            remote(vqkv.at[1:3], kv.at[:, slot_own, 0:TV], to),
            remote(aqkv.at[1:3], kv.at[:, slot_own, TV:TT], to),
        ]

    r_cot = {k: remote(cot_hbm, cotb.at[zr], z_peer(k)) for k in (2, 6)}
    r_kv = {k: send_kv(y_peer(k)) for k in (1, 3, 2)}
    w_rows = pl.ds(pl.multiple_of(core * 64, 64), 64)
    wp_rows = pl.ds(pl.multiple_of(HD + core * 64, 64), 64)
    r_w = remote(w_hbm.at[w_rows, other_cols], wp.at[wp_rows], cross)
    r_q = [remote(vqkv.at[0], q.at[xv], partner), remote(aqkv.at[0], q.at[xa], partner)]
    for k in (3, 5, 1, 7):
        r_cot[k] = remote(cot_hbm, cotb.at[zr], z_peer(k))
    r_sib = send_kv(sibling)
    r_ga = remote(acot_hbm, gb.at[xa], partner)

    rate = slope_ref[0] * LOG2E
    low1 = low_half(1)
    lane = lax.broadcasted_iota(jnp.int32, (1, QV), 1)
    lane_slot = lax.shift_right_logical(lane, 7)
    lane_frame = lax.shift_right_logical(lane, 6) - 2 * lane_slot
    query_frame_v = (8 * y + 4 * lane_slot + 2 * core + lane_frame).astype(F32)
    first = frame_ref[pl.ds(2 * y, 1), :].astype(F32)
    second = frame_ref[pl.ds(2 * y + 1, 1), :].astype(F32)
    query_frame_a = jnp.where(
        core == 0,
        jnp.where(low1, first, roll64(second)),
        jnp.where(low1, roll64(first), second),
    )
    row_frame = lax.shift_right_logical(lax.broadcasted_iota(jnp.int32, (TV, 1), 0), 6)
    for slot in range(NY):
        one = frame_ref[pl.ds(2 * slot + x_hi, 1), :].astype(F32)
        turned = jnp.broadcast_to(one, (128, 128)).T
        for c in range(2):
            frame_v = (8 * slot + 4 * x_hi + 2 * c + row_frame).astype(F32)
            bias_v[NY * c + slot] = rate * jnp.abs(frame_v - query_frame_a)
            frame_a = turned[64 * c : 64 * (c + 1), 0:1]
            bias_a[NY * c + slot] = rate * jnp.abs(frame_a - query_frame_v)

    for k in (1, 3):
        for copy in r_kv[k]:
            copy.wait_recv()
        at = NY * core + y_slot(NY - k)
        r_sib.append(remote(kv.at[:, at], kv.at[:, at], sibling))
    r_far = []
    for k, half in ((2, 0), (6, 1)):
        r_cot[k].wait_recv()
        rows = pl.ds(pl.multiple_of(z_slot(NZ - k) * COLS + half * 96, 32), 96)
        r_far.append(remote(cotb.at[rows], cotb.at[rows], z_peer(k)))
    l_w.wait()
    wpt[:, 0:HD] = wp[0:HD, :].T
    r_w.wait_recv()
    r_w2 = remote(wp.at[wp_rows], wp.at[wp_rows], sibling)
    for copy in r_kv[2]:
        copy.wait_recv()
    at = NY * core + y_slot(2)
    r_sib.append(remote(kv.at[:, at], kv.at[:, at], sibling))

    l_cot.wait()
    for k in (3, 5, 1, 7):
        r_cot[k].wait_recv()
    for copy in r_far:
        copy.wait_recv()
    r_w2.wait_recv()
    cot_all = cotb[...]
    gp_send[...] = mm(wp[HD : 2 * HD, :], cot_all).astype(BF)
    r_gp = remote(gp_send, gp_recv, cross)
    r_gd = remote(gp_send, gd_recv, corner)
    go_send[...] = mm(wp[0:HD, :], cot_all).astype(BF)
    r_go = remote(go_send, go_recv, partner)
    wpt[:, HD : 2 * HD] = wp[HD : 2 * HD, :].T

    l_kvv.wait()
    l_kva.wait()
    l_qv.wait()
    l_qa.wait()
    for copy in r_q + r_sib:
        copy.wait_recv()
    c2 = HD ** (-0.5) * LOG2E
    keys = kv[0].reshape(NS * TT, HD)
    values_t = kv[1].reshape(NS * TT, HD).T
    for c, cols in enumerate((slice(0, QV), slice(QV, QT))):
        wide = cols.stop - cols.start
        scores = (mm(keys, q[cols, :], NT) * c2).reshape(NS, TT, wide)
        part_v, part_a = scores[:, 0:TV], scores[:, TV:TT]
        if c == 0:
            part_a = part_a - bias_a[...]
        else:
            part_v = part_v - bias_v[...]
        high = jnp.maximum(
            jnp.max(part_v.reshape(NS * TV, wide), axis=0, keepdims=True),
            jnp.max(part_a.reshape(NS * TA, wide), axis=0, keepdims=True),
        )
        part_v = jnp.exp2(part_v - high)
        part_a = jnp.exp2(part_a - high)
        total = jnp.sum(part_v.reshape(NS * TV, wide), axis=0, keepdims=True) + jnp.sum(
            part_a.reshape(NS * TA, wide), axis=0, keepdims=True
        )
        p_scr[:, 0:TV, cols] = part_v
        p_scr[:, TV:TT, cols] = part_a
        probs = jnp.concatenate([part_v, part_a], axis=1).reshape(NS * TT, wide).astype(BF)
        mixed = mm(values_t, probs).T.astype(BF)
        rows_each = wide // 2
        for owner in range(2):
            piece = mixed[rows_each * owner : rows_each * (owner + 1)]
            if c == 0:
                osend[owner, 0:TV] = piece
            else:
                osend[owner, TV:TT] = piece
        st_send[0:1, cols] = high
        st_send[1:2, cols] = total
    r_st = [remote(st_send, st_recv.at[n], to) for n, to in enumerate((partner, cross, corner))]
    r_o = [
        remote(osend.at[1 - x_hi], orecv, partner),
        remote(osend.at[x_hi, 0:TV], oc_recv, cross),
        remote(osend.at[1 - x_hi, 0:TV], od_recv, corner),
    ]

    r_gp.wait_recv()
    grad_t = (go_send[...].astype(F32) + gp_recv[...].astype(F32)).astype(BF).astype(F32)
    gb[xv, :] = grad_t.T.astype(BF)
    r_go.wait_recv()
    r_gd.wait_recv()
    grad_o = go_recv[...].astype(F32) + gd_recv[...].astype(F32)
    xv_other = pl.ds(pl.multiple_of((1 - x_hi) * TV, TV), TV)
    gb[xv_other, :] = grad_o.T.astype(BF)

    for copy in r_st:
        copy.wait_recv()

    def shares(first, second):
        top = jnp.maximum(first[0:1, :], second[0:1, :])
        e_first = jnp.exp2(first[0:1, :] - top)
        e_second = jnp.exp2(second[0:1, :] - top)
        norm = first[1:2, :] * e_first + second[1:2, :] * e_second
        return e_first / norm, e_second / norm

    own_factor, other_factor = shares(st_send, st_recv[0])
    col_scr[0:1, :] = own_factor
    col_scr[1:2, :] = other_factor
    cross_factor, corner_factor = shares(st_recv[1], st_recv[2])
    col_scr[2:3, :] = cross_factor
    col_scr[3:4, :] = corner_factor

    pad = jnp.zeros((120, 128), F32)
    turned_v = jnp.concatenate([col_scr[:, xv], pad], axis=0).T
    turned_a = jnp.concatenate([col_scr[:, QV:QT], pad], axis=0).T
    turned_a = jnp.where(x_hi == 1, turned_a[64:128], turned_a[0:64])
    for copy in r_o:
        copy.wait_recv()
    mine, other = osend[x_hi].astype(F32), orecv[...].astype(F32)
    mix_v = mine[0:TV] * turned_v[:, 0:1] + other[0:TV] * turned_v[:, 1:2]
    mix_a = mine[TV:TT] * turned_a[:, 0:1] + other[TV:TT] * turned_a[:, 1:2]
    mix_vb = mix_v.astype(BF)
    mix_ab = mix_a.astype(BF)
    mix_c = oc_recv[...].astype(F32) * turned_v[:, 2:3] + od_recv[...].astype(F32) * turned_v[:, 3:4]
    res_ref[COLS : COLS + TA, :] = mix_ab
    l_ga.wait()
    dot_a = jnp.sum(
        jnp.concatenate(
            [gb[xa, :].astype(F32) * mix_ab.astype(F32), jnp.zeros((64, 128), F32)], axis=0
        ).T,
        axis=0,
        keepdims=True,
    )
    dot_v = jnp.sum(grad_t * mix_vb.astype(F32).T, axis=0, keepdims=True)
    dot_buf[x_hi, 0:1, 0:128] = dot_v
    dot_buf[x_hi, 0:1, 128:256] = dot_a
    r_dot = remote(dot_buf.at[x_hi], dot_buf.at[x_hi], partner)

    both = jnp.concatenate([mix_vb, mix_c.astype(BF)], axis=1)
    os[...] = mm(wpt[...], both, NT).astype(BF).reshape(NZ, COLS, HD)
    r_ofar = [
        remote(os.at[z_slot(4), 96 * half : 96 * (half + 1)], ofar_recv.at[half], z_peer(k))
        for k, half in ((2, 0), (6, 1))
    ]
    r_os = {k: remote(os.at[z_slot(k)], orx.at[k - 1], z_peer(k)) for k in (3, 5, 1, 7)}

    r_ga.wait_recv()
    order = ((0, 2), (0, 1), (0, 3), (0, 0), (1, 2), (1, 1), (1, 3), (1, 0))
    r_half, r_dkv = {}, []

    def hand_over(part, mine, k, value):
        if not mine:
            sib_send[k, part] = value.astype(BF)
            r_half[part, k] = remote(sib_send.at[k, part], sib_recv.at[k, part], sibling)
        elif k:
            r_half[part, k].wait_recv()
            dkv_send[k - 1, part] = (value + sib_recv[k, part].astype(F32)).astype(BF)
            r_dkv.append(
                remote(dkv_send.at[k - 1, part], dkv_recv.at[k - 1, part], y_peer(k))
            )
        else:
            dkv_own[part] = value

    def slot_of(mine, k):
        return NY * (core if mine else 1 - core) + y_slot(k)

    for mine, k in order:
        slot = slot_of(mine, k)
        prob = p_scr[slot] * own_factor
        p_scr[slot] = prob
        hand_over(1, mine, k, mm(prob.astype(BF), gb[...]))

    r_dot.wait_recv()
    dots = [dot_buf[k, 0:1, :] for k in range(2)]
    dot = jnp.concatenate(
        [dots[0][:, 0:128], dots[1][:, 0:128]]
        + [jnp.where(low1, dots[0][:, 128:256], roll64(dots[1][:, 128:256]))],
        axis=1,
    )
    c = HD ** (-0.5)
    dq_t = jnp.zeros((HD, QT), F32)
    for mine, k in order:
        slot = slot_of(mine, k)
        dp = mm(kv[1, slot], gb[...], NT)
        ds = (p_scr[slot] * (dp - dot)).astype(BF)
        hand_over(0, mine, k, mm(ds, q[...]) * c)
        dq_t = dq_t + mm(kv[0, slot].T, ds)
        if (mine, k) == (0, 0):
            for at, half in ((2, 0), (6, 1)):
                r_ofar[half].wait_recv()
                rows = slice(96 * half, 96 * (half + 1))
                share = os[z_slot(at), rows].astype(F32) + ofar_recv[half].astype(F32)
                ofar[half, rows] = share.astype(BF)
                rest = slice(96 * (1 - half), 96 * (2 - half))
                ofar[half, rest] = os[z_slot(at), rest]
                r_os[at] = remote(ofar.at[half], orx.at[at - 1], z_peer(at))
    dq = (dq_t * c).T.astype(BF)
    for owner in range(2):
        dq_send[owner, 0:TV] = dq[TV * owner : TV * (owner + 1)]
        dq_send[owner, TV:TT] = dq[QV + TA * owner : QV + TA * (owner + 1)]
    r_dq = remote(dq_send.at[1 - x_hi], dq_recv, partner)

    total = os[z].astype(F32)
    for k in (3, 5, 1, 7, 2, 6):
        r_os[k].wait_recv()
        total = total + orx[k - 1].astype(F32)
    res_ref[0:COLS, :] = total.astype(BF)
    r_half[0, 0].wait_recv()
    r_half[1, 0].wait_recv()
    dkv = dkv_own[...] + sib_recv[0].astype(F32)
    for copy in r_dkv:
        copy.wait_recv()
    for k in range(3):
        dkv = dkv + dkv_recv[k].astype(F32)
    dkv = dkv.astype(BF)
    for n in range(2):
        res_ref[AT_V + TV * (n + 1) : AT_V + TV * (n + 2), :] = dkv[n, 0:TV]
        res_ref[AT_A + TA * (n + 1) : AT_A + TA * (n + 2), :] = dkv[n, TV:TT]
    r_dq.wait_recv()
    dq = (dq_send[x_hi].astype(F32) + dq_recv[...].astype(F32)).astype(BF)
    res_ref[AT_V : AT_V + TV, :] = dq[0:TV]
    res_ref[AT_A : AT_A + TA, :] = dq[TV:TT]
    for copy in sends:
        copy.wait_send()


def unpack(res, out_ref, amix_ref, vgrad_ref, agrad_ref):
    out_ref[...] = res[0:COLS, :]
    amix_ref[...] = res[COLS : COLS + TA, :]
    vgrad_ref[...] = res[AT_V:AT_A, :].reshape(3, TV, HD)
    agrad_ref[...] = res[AT_A : AT_A + 3 * TA, :].reshape(3, TA, HD)


def per_device(video_qkv, audio_qkv, head_slopes, audio_frame, out_weight, video_cot, audio_cot):
    any_spec = pl.BlockSpec(memory_space=pl.ANY)
    vmem = pl.BlockSpec(memory_space=pltpu.VMEM)
    smem = pl.BlockSpec(memory_space=pltpu.SMEM)
    scratch = [
        pltpu.VMEM((2, NS, TT, HD), BF),
        pltpu.VMEM((QT, HD), BF),
        pltpu.VMEM((QT, HD), BF),
        pltpu.VMEM((HALF, TV), BF),
        pltpu.VMEM((2 * HD, HALF), BF),
        pltpu.VMEM((HALF, 2 * HD), BF),
        pltpu.VMEM((NS, TV, QA), F32),
        pltpu.VMEM((NS, TA, QV), F32),
        pltpu.VMEM((NS, TT, QT), F32),
        pltpu.VMEM((2, TT, HD), BF),
        pltpu.VMEM((TT, HD), BF),
        pltpu.VMEM((TV, HD), BF),
        pltpu.VMEM((TV, HD), BF),
        pltpu.VMEM((8, QT), F32),
        pltpu.VMEM((3, 8, QT), F32),
        pltpu.VMEM((8, QT), F32),
        pltpu.VMEM((HD, TV), BF),
        pltpu.VMEM((HD, TV), BF),
        pltpu.VMEM((HD, TV), BF),
        pltpu.VMEM((HD, TV), BF),
        pltpu.VMEM((HD, TV), BF),
        pltpu.VMEM((2, 8, 256), F32),
        pltpu.VMEM((NZ, COLS, HD), BF),
        pltpu.VMEM((NZ - 1, COLS, HD), BF),
        pltpu.VMEM((2, COLS, HD), BF),
        pltpu.VMEM((2, COLS // 2, HD), BF),
        pltpu.VMEM((NY, 2, TT, HD), BF),
        pltpu.VMEM((NY, 2, TT, HD), BF),
        pltpu.VMEM((3, 2, TT, HD), BF),
        pltpu.VMEM((3, 2, TT, HD), BF),
        pltpu.VMEM((2, TT, HD), F32),
        pltpu.VMEM((2, TT, HD), BF),
        pltpu.VMEM((TT, HD), BF),
        pltpu.SemaphoreType.DMA((8,)),
        pltpu.SemaphoreType.DMA((64,)),
        pltpu.SemaphoreType.DMA((64,)),
    ]
    res = pl.pallas_call(
        kernel,
        out_shape=jax.ShapeDtypeStruct((AT_A + 3 * TA, HD), BF),
        in_specs=[any_spec, any_spec, smem, vmem, any_spec, any_spec, any_spec],
        out_specs=vmem,
        scratch_shapes=scratch,
        compiler_params=pltpu.CompilerParams(
            collective_id=0, has_side_effects=True, vmem_limit_bytes=56 * 1024 * 1024
        ),
    )(
        video_qkv,
        audio_qkv,
        head_slopes,
        audio_frame.reshape(8, 128),
        out_weight,
        video_cot.T,
        audio_cot,
    )
    out_t, audio_mix, video_grad, audio_grad = pl.pallas_call(
        unpack,
        out_shape=(
            jax.ShapeDtypeStruct((COLS, TV), BF),
            jax.ShapeDtypeStruct((TA, HD), BF),
            jax.ShapeDtypeStruct((3, TV, HD), BF),
            jax.ShapeDtypeStruct((3, TA, HD), BF),
        ),
        in_specs=[vmem],
        out_specs=(vmem,) * 4,
    )(res)
    return out_t.T, audio_mix, video_grad, audio_grad


def solution(mesh):
    in_specs = (
        P(None, "seq", "grp"),
        P(None, "seq", "grp"),
        P("grp"),
        P(),
        P("grp", None),
        P("seq", "grp"),
        P("seq", "grp"),
    )
    out_specs = (P("seq", "grp"), P("seq", "grp"), P(None, "seq", "grp"), P(None, "seq", "grp"))
    return jax.shard_map(
        per_device, mesh=mesh, in_specs=in_specs, out_specs=out_specs, check_vma=False
    )
```

```python
import math

import jax
import jax.numpy as jnp
from jax import lax
from jax.experimental import pallas as pl
from jax.experimental.pallas import tpu as pltpu
from jax.sharding import PartitionSpec as P

BF = jnp.bfloat16
F32 = jnp.float32
HD = 128
TV = 128
TA = 64
TT = TV + TA
NY = 4
NS = 2 * NY
NZ = 8
QV = 2 * TV
QA = 2 * TA
QT = QV + QA
COLS = 192
HALF = NZ * COLS
LOG2E = 1.4426950408889634
AT_V = COLS + TA
AT_A = AT_V + 3 * TV

NN = (((1,), (0,)), ((), ()))
NT = (((1,), (1,)), ((), ()))


def mm(a, b, dims=NN):
    return lax.dot_general(a, b, dims, preferred_element_type=F32)


def roll64(x):
    return pltpu.roll(x, 64, 1)


def low_half(rows):
    return lax.broadcasted_iota(jnp.int32, (rows, 128), 1) < 64


def kernel(
    vqkv, aqkv, slope_ref, frame_ref, w_hbm, cot_hbm, acot_hbm,
    res_ref,
    kv, q, gb, cotb, wp, wpt, bias_v, bias_a, p_scr,
    osend, orecv, oc_recv, od_recv, sv_send, sv_recv, sa_send, sa_recv, col_scr,
    gp_send, gp_recv, go_send, go_recv, gd_recv, dot_buf, os, orx, ofar, ofar_recv,
    sib_send, sib_recv, dkv_send, dkv_recv, dkv_own, dq_send, dq_recv,
    lsem, ssem, rsem,
):
    s = lax.axis_index("seq")
    grp = lax.axis_index("grp")
    y = lax.div(s, 4)
    x_hi = lax.div(lax.rem(s, 4), 2)
    core = lax.rem(s, 2)
    x_lo = lax.div(grp, NZ)
    z = lax.rem(grp, NZ)
    sibling = (s + 1 - 2 * core, grp)
    partner = (s + 2 - 4 * x_hi, grp)
    cross = (s, lax.rem(grp + NZ, 2 * NZ))
    corner = (s + 2 - 4 * x_hi, lax.rem(grp + NZ, 2 * NZ))

    def y_slot(k):
        return lax.rem(y + k, NY)

    def y_peer(k):
        return (lax.rem(s + 4 * k, 4 * NY), grp)

    def z_slot(k):
        return lax.rem(z + k, NZ)

    def z_peer(k):
        return (s, x_lo * NZ + z_slot(k))

    sends = []
    count = [0]

    def remote(src, dst, to):
        i = count[0]
        count[0] += 1
        copy = pltpu.make_async_remote_copy(
            src_ref=src,
            dst_ref=dst,
            send_sem=ssem.at[i],
            recv_sem=rsem.at[i],
            device_id=to,
            device_id_type=pl.DeviceIdType.MESH,
        )
        copy.start()
        sends.append(copy)
        return copy

    local_count = [0]

    def local(src, dst):
        i = local_count[0]
        local_count[0] += 1
        copy = pltpu.make_async_copy(src, dst, lsem.at[i])
        copy.start()
        return copy

    barrier = pltpu.get_barrier_semaphore()
    peers = (
        [z_peer(k) for k in range(1, NZ)]
        + [cross, corner, sibling, partner]
        + [y_peer(k) for k in range(1, NY)]
    )
    for peer in peers:
        pl.semaphore_signal(barrier, inc=1, device_id=peer, device_id_type=pl.DeviceIdType.MESH)

    xv = pl.ds(pl.multiple_of(x_hi * TV, TV), TV)
    xa = pl.ds(pl.multiple_of(QV + x_hi * TA, TA), TA)
    zr = pl.ds(pl.multiple_of(z * COLS, 64), COLS)
    own_cols = pl.ds(pl.multiple_of(x_lo * HALF, HALF), HALF)
    other_cols = pl.ds(pl.multiple_of((1 - x_lo) * HALF, HALF), HALF)
    slot_own = NY * core + y
    l_cot = local(cot_hbm, cotb.at[zr])
    l_w = local(w_hbm.at[:, own_cols], wp.at[0:HD])
    l_kvv = local(vqkv.at[1:3], kv.at[:, slot_own, 0:TV])
    l_kva = local(aqkv.at[1:3], kv.at[:, slot_own, TV:TT])
    l_qv = local(vqkv.at[0], q.at[xv])
    l_qa = local(aqkv.at[0], q.at[xa])
    l_ga = local(acot_hbm, gb.at[xa])

    pl.semaphore_wait(barrier, len(peers))

    def send_kv(to):
        return [
            remote(vqkv.at[1:3], kv.at[:, slot_own, 0:TV], to),
            remote(aqkv.at[1:3], kv.at[:, slot_own, TV:TT], to),
        ]

    r_cot = {k: remote(cot_hbm, cotb.at[zr], z_peer(k)) for k in (2, 6)}
    r_kv = {k: send_kv(y_peer(k)) for k in (1, 3, 2)}
    w_rows = pl.ds(pl.multiple_of(core * 64, 64), 64)
    wp_rows = pl.ds(pl.multiple_of(HD + core * 64, 64), 64)
    r_w = remote(w_hbm.at[w_rows, other_cols], wp.at[wp_rows], cross)
    r_q = [remote(vqkv.at[0], q.at[xv], partner), remote(aqkv.at[0], q.at[xa], partner)]
    for k in (3, 5, 1, 7):
        r_cot[k] = remote(cot_hbm, cotb.at[zr], z_peer(k))
    r_sib = send_kv(sibling)
    r_ga = remote(acot_hbm, gb.at[xa], partner)

    rate = slope_ref[0] * LOG2E
    low1 = low_half(1)
    lane = lax.broadcasted_iota(jnp.int32, (1, QV), 1)
    lane_slot = lax.shift_right_logical(lane, 7)
    lane_frame = lax.shift_right_logical(lane, 6) - 2 * lane_slot
    query_frame_v = (8 * y + 4 * lane_slot + 2 * core + lane_frame).astype(F32)
    first = frame_ref[pl.ds(2 * y, 1), :].astype(F32)
    second = frame_ref[pl.ds(2 * y + 1, 1), :].astype(F32)
    query_frame_a = jnp.where(
        core == 0,
        jnp.where(low1, first, roll64(second)),
        jnp.where(low1, roll64(first), second),
    )
    row_frame = lax.shift_right_logical(lax.broadcasted_iota(jnp.int32, (TV, 1), 0), 6)
    for slot in range(NY):
        one = frame_ref[pl.ds(2 * slot + x_hi, 1), :].astype(F32)
        turned = jnp.broadcast_to(one, (128, 128)).T
        for c in range(2):
            frame_v = (8 * slot + 4 * x_hi + 2 * c + row_frame).astype(F32)
            bias_v[NY * c + slot] = rate * jnp.abs(frame_v - query_frame_a)
            frame_a = turned[64 * c : 64 * (c + 1), 0:1]
            bias_a[NY * c + slot] = rate * jnp.abs(frame_a - query_frame_v)

    for k in (1, 3):
        for copy in r_kv[k]:
            copy.wait_recv()
        at = NY * core + y_slot(NY - k)
        r_sib.append(remote(kv.at[:, at], kv.at[:, at], sibling))
    r_far = []
    for k, half in ((2, 0), (6, 1)):
        r_cot[k].wait_recv()
        rows = pl.ds(pl.multiple_of(z_slot(NZ - k) * COLS + half * 96, 32), 96)
        r_far.append(remote(cotb.at[rows], cotb.at[rows], z_peer(k)))
    l_w.wait()
    wpt[:, 0:HD] = wp[0:HD, :].T
    r_w.wait_recv()
    r_w2 = remote(wp.at[wp_rows], wp.at[wp_rows], sibling)
    for copy in r_kv[2]:
        copy.wait_recv()
    at = NY * core + y_slot(2)
    r_sib.append(remote(kv.at[:, at], kv.at[:, at], sibling))

    l_kvv.wait()
    l_kva.wait()
    l_qv.wait()
    l_qa.wait()
    for copy in r_q + r_sib:
        copy.wait_recv()
    c2 = HD ** (-0.5) * LOG2E
    keys = kv[0].reshape(NS * TT, HD)
    values_t = kv[1].reshape(NS * TT, HD).T
    for c, cols in enumerate((slice(0, QV), slice(QV, QT))):
        wide = cols.stop - cols.start
        scores = (mm(keys, q[cols, :], NT) * c2).reshape(NS, TT, wide)
        part_v, part_a = scores[:, 0:TV], scores[:, TV:TT]
        if c == 0:
            part_a = part_a - bias_a[...]
        else:
            part_v = part_v - bias_v[...]
        high = jnp.maximum(
            jnp.max(part_v.reshape(NS * TV, wide), axis=0, keepdims=True),
            jnp.max(part_a.reshape(NS * TA, wide), axis=0, keepdims=True),
        )
        part_v = jnp.exp2(part_v - high)
        part_a = jnp.exp2(part_a - high)
        total = jnp.sum(part_v.reshape(NS * TV, wide), axis=0, keepdims=True) + jnp.sum(
            part_a.reshape(NS * TA, wide), axis=0, keepdims=True
        )
        p_scr[:, 0:TV, cols] = part_v
        p_scr[:, TV:TT, cols] = part_a
        probs = jnp.concatenate([part_v, part_a], axis=1).reshape(NS * TT, wide).astype(BF)
        mixed = mm(values_t, probs).T.astype(BF)
        rows_each = wide // 2
        for owner in range(2):
            piece = mixed[rows_each * owner : rows_each * (owner + 1)]
            if c == 0:
                osend[owner, 0:TV] = piece
            else:
                osend[owner, TV:TT] = piece
        if c == 0:
            sv_send[0:1, :] = high
            sv_send[1:2, :] = total
            r_sv = [
                remote(sv_send, sv_recv.at[n], to) for n, to in enumerate((partner, cross, corner))
            ]
            r_o = [
                remote(osend.at[1 - x_hi, 0:TV], orecv.at[0:TV], partner),
                remote(osend.at[x_hi, 0:TV], oc_recv, cross),
                remote(osend.at[1 - x_hi, 0:TV], od_recv, corner),
            ]
        else:
            sa_send[0:1, :] = high
            sa_send[1:2, :] = total
            r_sa = remote(sa_send, sa_recv, partner)
            r_oa = remote(osend.at[1 - x_hi, TV:TT], orecv.at[TV:TT], partner)

    l_cot.wait()
    for k in (3, 5, 1, 7):
        r_cot[k].wait_recv()
    for copy in r_far:
        copy.wait_recv()
    r_w2.wait_recv()
    cot_all = cotb[...]
    gp_send[...] = mm(wp[HD : 2 * HD, :], cot_all).astype(BF)
    r_gp = remote(gp_send, gp_recv, cross)
    r_gd = remote(gp_send, gd_recv, corner)
    go_send[...] = mm(wp[0:HD, :], cot_all).astype(BF)
    r_go = remote(go_send, go_recv, partner)
    wpt[:, HD : 2 * HD] = wp[HD : 2 * HD, :].T

    for copy in r_sv:
        copy.wait_recv()

    def shares(first, second):
        top = jnp.maximum(first[0:1, :], second[0:1, :])
        e_first = jnp.exp2(first[0:1, :] - top)
        e_second = jnp.exp2(second[0:1, :] - top)
        norm = first[1:2, :] * e_first + second[1:2, :] * e_second
        return e_first / norm, e_second / norm

    own_v, other_v = shares(sv_send, sv_recv[0])
    col_scr[0:1, 0:QV] = own_v
    col_scr[1:2, 0:QV] = other_v
    cross_v, corner_v = shares(sv_recv[1], sv_recv[2])
    col_scr[2:3, 0:QV] = cross_v
    col_scr[3:4, 0:QV] = corner_v

    pad = jnp.zeros((120, 128), F32)
    turned_v = jnp.concatenate([col_scr[:, xv], pad], axis=0).T
    for copy in r_o:
        copy.wait_recv()
    mine, other = osend[x_hi, 0:TV].astype(F32), orecv[0:TV].astype(F32)
    mix_vb = (mine * turned_v[:, 0:1] + other * turned_v[:, 1:2]).astype(BF)
    mix_c = oc_recv[...].astype(F32) * turned_v[:, 2:3] + od_recv[...].astype(F32) * turned_v[:, 3:4]

    both = jnp.concatenate([mix_vb, mix_c.astype(BF)], axis=1)
    os[...] = mm(wpt[...], both, NT).astype(BF).reshape(NZ, COLS, HD)
    r_ofar = [
        remote(os.at[z_slot(4), 96 * half : 96 * (half + 1)], ofar_recv.at[half], z_peer(k))
        for k, half in ((2, 0), (6, 1))
    ]
    r_os = {k: remote(os.at[z_slot(k)], orx.at[k - 1], z_peer(k)) for k in (3, 5, 1, 7)}

    r_gp.wait_recv()
    grad_t = (go_send[...].astype(F32) + gp_recv[...].astype(F32)).astype(BF).astype(F32)
    gb[xv, :] = grad_t.T.astype(BF)
    r_go.wait_recv()
    r_gd.wait_recv()
    grad_o = go_recv[...].astype(F32) + gd_recv[...].astype(F32)
    xv_other = pl.ds(pl.multiple_of((1 - x_hi) * TV, TV), TV)
    gb[xv_other, :] = grad_o.T.astype(BF)

    r_sa.wait_recv()
    own_a, other_a = shares(sa_send, sa_recv)
    own_factor = jnp.concatenate([own_v, own_a], axis=1)
    col_scr[0:1, QV:QT] = own_a
    col_scr[1:2, QV:QT] = other_a
    turned_a = jnp.concatenate([col_scr[:, QV:QT], pad], axis=0).T
    turned_a = jnp.where(x_hi == 1, turned_a[64:128], turned_a[0:64])
    r_oa.wait_recv()
    mine, other = osend[x_hi, TV:TT].astype(F32), orecv[TV:TT].astype(F32)
    mix_ab = (mine * turned_a[:, 0:1] + other * turned_a[:, 1:2]).astype(BF)
    res_ref[COLS : COLS + TA, :] = mix_ab
    l_ga.wait()
    dot_a = jnp.sum(
        jnp.concatenate(
            [gb[xa, :].astype(F32) * mix_ab.astype(F32), jnp.zeros((64, 128), F32)], axis=0
        ).T,
        axis=0,
        keepdims=True,
    )
    dot_v = jnp.sum(grad_t * mix_vb.astype(F32).T, axis=0, keepdims=True)
    dot_buf[x_hi, 0:1, 0:128] = dot_v
    dot_buf[x_hi, 0:1, 128:256] = dot_a
    r_dot = remote(dot_buf.at[x_hi], dot_buf.at[x_hi], partner)

    r_ga.wait_recv()
    order = ((0, 2), (0, 1), (0, 3), (0, 0), (1, 2), (1, 1), (1, 3), (1, 0))
    r_half, r_dkv = {}, []

    def hand_over(part, mine, k, value):
        if not mine:
            sib_send[k, part] = value.astype(BF)
            r_half[part, k] = remote(sib_send.at[k, part], sib_recv.at[k, part], sibling)
        elif k:
            r_half[part, k].wait_recv()
            dkv_send[k - 1, part] = (value + sib_recv[k, part].astype(F32)).astype(BF)
            r_dkv.append(
                remote(dkv_send.at[k - 1, part], dkv_recv.at[k - 1, part], y_peer(k))
            )
        else:
            dkv_own[part] = value

    def slot_of(mine, k):
        return NY * (core if mine else 1 - core) + y_slot(k)

    for mine, k in order:
        slot = slot_of(mine, k)
        prob = p_scr[slot] * own_factor
        p_scr[slot] = prob
        hand_over(1, mine, k, mm(prob.astype(BF), gb[...]))

    for at, half in ((2, 0), (6, 1)):
        r_ofar[half].wait_recv()
        rows = slice(96 * half, 96 * (half + 1))
        share = os[z_slot(at), rows].astype(F32) + ofar_recv[half].astype(F32)
        ofar[half, rows] = share.astype(BF)
        rest = slice(96 * (1 - half), 96 * (2 - half))
        ofar[half, rest] = os[z_slot(at), rest]
        r_os[at] = remote(ofar.at[half], orx.at[at - 1], z_peer(at))

    r_dot.wait_recv()
    dots = [dot_buf[k, 0:1, :] for k in range(2)]
    dot = jnp.concatenate(
        [dots[0][:, 0:128], dots[1][:, 0:128]]
        + [jnp.where(low1, dots[0][:, 128:256], roll64(dots[1][:, 128:256]))],
        axis=1,
    )
    c = HD ** (-0.5)
    dq_t = jnp.zeros((HD, QT), F32)
    for mine, k in order:
        slot = slot_of(mine, k)
        dp = mm(kv[1, slot], gb[...], NT)
        ds = (p_scr[slot] * (dp - dot)).astype(BF)
        hand_over(0, mine, k, mm(ds, q[...]) * c)
        dq_t = dq_t + mm(kv[0, slot].T, ds)
    dq = (dq_t * c).T.astype(BF)
    for owner in range(2):
        dq_send[owner, 0:TV] = dq[TV * owner : TV * (owner + 1)]
        dq_send[owner, TV:TT] = dq[QV + TA * owner : QV + TA * (owner + 1)]
    r_dq = remote(dq_send.at[1 - x_hi], dq_recv, partner)

    total = os[z].astype(F32)
    for k in (3, 5, 1, 7, 2, 6):
        r_os[k].wait_recv()
        total = total + orx[k - 1].astype(F32)
    res_ref[0:COLS, :] = total.astype(BF)
    r_half[0, 0].wait_recv()
    r_half[1, 0].wait_recv()
    dkv = dkv_own[...] + sib_recv[0].astype(F32)
    for copy in r_dkv:
        copy.wait_recv()
    for k in range(3):
        dkv = dkv + dkv_recv[k].astype(F32)
    dkv = dkv.astype(BF)
    for n in range(2):
        res_ref[AT_V + TV * (n + 1) : AT_V + TV * (n + 2), :] = dkv[n, 0:TV]
        res_ref[AT_A + TA * (n + 1) : AT_A + TA * (n + 2), :] = dkv[n, TV:TT]
    r_dq.wait_recv()
    dq = (dq_send[x_hi].astype(F32) + dq_recv[...].astype(F32)).astype(BF)
    res_ref[AT_V : AT_V + TV, :] = dq[0:TV]
    res_ref[AT_A : AT_A + TA, :] = dq[TV:TT]
    for copy in sends:
        copy.wait_send()


def unpack(res, out_ref, amix_ref, vgrad_ref, agrad_ref):
    out_ref[...] = res[0:COLS, :]
    amix_ref[...] = res[COLS : COLS + TA, :]
    vgrad_ref[...] = res[AT_V:AT_A, :].reshape(3, TV, HD)
    agrad_ref[...] = res[AT_A : AT_A + 3 * TA, :].reshape(3, TA, HD)


def per_device(video_qkv, audio_qkv, head_slopes, audio_frame, out_weight, video_cot, audio_cot):
    any_spec = pl.BlockSpec(memory_space=pl.ANY)
    vmem = pl.BlockSpec(memory_space=pltpu.VMEM)
    smem = pl.BlockSpec(memory_space=pltpu.SMEM)
    scratch = [
        pltpu.VMEM((2, NS, TT, HD), BF),
        pltpu.VMEM((QT, HD), BF),
        pltpu.VMEM((QT, HD), BF),
        pltpu.VMEM((HALF, TV), BF),
        pltpu.VMEM((2 * HD, HALF), BF),
        pltpu.VMEM((HALF, 2 * HD), BF),
        pltpu.VMEM((NS, TV, QA), F32),
        pltpu.VMEM((NS, TA, QV), F32),
        pltpu.VMEM((NS, TT, QT), F32),
        pltpu.VMEM((2, TT, HD), BF),
        pltpu.VMEM((TT, HD), BF),
        pltpu.VMEM((TV, HD), BF),
        pltpu.VMEM((TV, HD), BF),
        pltpu.VMEM((8, QV), F32),
        pltpu.VMEM((3, 8, QV), F32),
        pltpu.VMEM((8, QA), F32),
        pltpu.VMEM((8, QA), F32),
        pltpu.VMEM((8, QT), F32),
        pltpu.VMEM((HD, TV), BF),
        pltpu.VMEM((HD, TV), BF),
        pltpu.VMEM((HD, TV), BF),
        pltpu.VMEM((HD, TV), BF),
        pltpu.VMEM((HD, TV), BF),
        pltpu.VMEM((2, 8, 256), F32),
        pltpu.VMEM((NZ, COLS, HD), BF),
        pltpu.VMEM((NZ - 1, COLS, HD), BF),
        pltpu.VMEM((2, COLS, HD), BF),
        pltpu.VMEM((2, COLS // 2, HD), BF),
        pltpu.VMEM((NY, 2, TT, HD), BF),
        pltpu.VMEM((NY, 2, TT, HD), BF),
        pltpu.VMEM((3, 2, TT, HD), BF),
        pltpu.VMEM((3, 2, TT, HD), BF),
        pltpu.VMEM((2, TT, HD), F32),
        pltpu.VMEM((2, TT, HD), BF),
        pltpu.VMEM((TT, HD), BF),
        pltpu.SemaphoreType.DMA((8,)),
        pltpu.SemaphoreType.DMA((64,)),
        pltpu.SemaphoreType.DMA((64,)),
    ]
    res = pl.pallas_call(
        kernel,
        out_shape=jax.ShapeDtypeStruct((AT_A + 3 * TA, HD), BF),
        in_specs=[any_spec, any_spec, smem, vmem, any_spec, any_spec, any_spec],
        out_specs=vmem,
        scratch_shapes=scratch,
        compiler_params=pltpu.CompilerParams(
            collective_id=0, has_side_effects=True, vmem_limit_bytes=56 * 1024 * 1024
        ),
    )(
        video_qkv,
        audio_qkv,
        head_slopes,
        audio_frame.reshape(8, 128),
        out_weight,
        video_cot.T,
        audio_cot,
    )
    out_t, audio_mix, video_grad, audio_grad = pl.pallas_call(
        unpack,
        out_shape=(
            jax.ShapeDtypeStruct((COLS, TV), BF),
            jax.ShapeDtypeStruct((TA, HD), BF),
            jax.ShapeDtypeStruct((3, TV, HD), BF),
            jax.ShapeDtypeStruct((3, TA, HD), BF),
        ),
        in_specs=[vmem],
        out_specs=(vmem,) * 4,
    )(res)
    return out_t.T, audio_mix, video_grad, audio_grad


def solution(mesh):
    in_specs = (
        P(None, "seq", "grp"),
        P(None, "seq", "grp"),
        P("grp"),
        P(),
        P("grp", None),
        P("seq", "grp"),
        P("seq", "grp"),
    )
    out_specs = (P("seq", "grp"), P("seq", "grp"), P(None, "seq", "grp"), P(None, "seq", "grp"))
    return jax.shard_map(
        per_device, mesh=mesh, in_specs=in_specs, out_specs=out_specs, check_vma=False
    )
```

```python
import math

import jax
import jax.numpy as jnp
from jax import lax
from jax.experimental import pallas as pl
from jax.experimental.pallas import tpu as pltpu
from jax.sharding import PartitionSpec as P

BF = jnp.bfloat16
F32 = jnp.float32
HD = 128
TV = 128
TA = 64
TT = TV + TA
NY = 4
NS = 2 * NY
NZ = 8
QV = 2 * TV
QA = 2 * TA
QT = QV + QA
COLS = 192
HALF = NZ * COLS
LOG2E = 1.4426950408889634
AT_V = COLS + TA
AT_A = AT_V + 3 * TV

NN = (((1,), (0,)), ((), ()))
NT = (((1,), (1,)), ((), ()))


def mm(a, b, dims=NN):
    return lax.dot_general(a, b, dims, preferred_element_type=F32)


def roll64(x):
    return pltpu.roll(x, 64, 1)


def low_half(rows):
    return lax.broadcasted_iota(jnp.int32, (rows, 128), 1) < 64


def kernel(
    vqkv, aqkv, slope_ref, frame_ref, w_hbm, cot_hbm, acot_hbm,
    res_ref,
    kv, q, gb, cotb, wp, wpt, bias_v, bias_a, p_scr,
    osend, orecv, oc_recv, od_recv, sv_send, sv_recv, sa_send, sa_recv, col_scr,
    gp_send, gp_recv, go_send, go_recv, gd_recv, dot_buf, os, orx, ofar, ofar_recv,
    sib_send, sib_recv, dkv_send, dkv_recv, dkv_own, dq_send, dq_recv,
    lsem, ssem, rsem,
):
    s = lax.axis_index("seq")
    grp = lax.axis_index("grp")
    y = lax.div(s, 4)
    x_hi = lax.div(lax.rem(s, 4), 2)
    core = lax.rem(s, 2)
    x_lo = lax.div(grp, NZ)
    z = lax.rem(grp, NZ)
    sibling = (s + 1 - 2 * core, grp)
    partner = (s + 2 - 4 * x_hi, grp)
    cross = (s, lax.rem(grp + NZ, 2 * NZ))
    corner = (s + 2 - 4 * x_hi, lax.rem(grp + NZ, 2 * NZ))

    def y_slot(k):
        return lax.rem(y + k, NY)

    def y_peer(k):
        return (lax.rem(s + 4 * k, 4 * NY), grp)

    def z_slot(k):
        return lax.rem(z + k, NZ)

    def z_peer(k):
        return (s, x_lo * NZ + z_slot(k))

    sends = []
    count = [0]

    def remote(src, dst, to):
        i = count[0]
        count[0] += 1
        copy = pltpu.make_async_remote_copy(
            src_ref=src,
            dst_ref=dst,
            send_sem=ssem.at[i],
            recv_sem=rsem.at[i],
            device_id=to,
            device_id_type=pl.DeviceIdType.MESH,
        )
        copy.start()
        sends.append(copy)
        return copy

    local_count = [0]

    def local(src, dst):
        i = local_count[0]
        local_count[0] += 1
        copy = pltpu.make_async_copy(src, dst, lsem.at[i])
        copy.start()
        return copy

    barrier = pltpu.get_barrier_semaphore()
    peers = (
        [z_peer(k) for k in range(1, NZ)]
        + [cross, corner, sibling, partner]
        + [y_peer(k) for k in range(1, NY)]
    )
    for peer in peers:
        pl.semaphore_signal(barrier, inc=1, device_id=peer, device_id_type=pl.DeviceIdType.MESH)

    xv = pl.ds(pl.multiple_of(x_hi * TV, TV), TV)
    xa = pl.ds(pl.multiple_of(QV + x_hi * TA, TA), TA)
    zr = pl.ds(pl.multiple_of(z * COLS, 64), COLS)
    own_cols = pl.ds(pl.multiple_of(x_lo * HALF, HALF), HALF)
    other_cols = pl.ds(pl.multiple_of((1 - x_lo) * HALF, HALF), HALF)
    slot_own = NY * core + y
    l_cot = local(cot_hbm, cotb.at[zr])
    l_w = local(w_hbm.at[:, own_cols], wp.at[0:HD])
    l_kvv = local(vqkv.at[1:3], kv.at[:, slot_own, 0:TV])
    l_kva = local(aqkv.at[1:3], kv.at[:, slot_own, TV:TT])
    l_qv = local(vqkv.at[0], q.at[xv])
    l_qa = local(aqkv.at[0], q.at[xa])
    l_ga = local(acot_hbm, gb.at[xa])

    pl.semaphore_wait(barrier, len(peers))

    def send_kv(to):
        return [
            remote(vqkv.at[1:3], kv.at[:, slot_own, 0:TV], to),
            remote(aqkv.at[1:3], kv.at[:, slot_own, TV:TT], to),
        ]

    r_cot = {k: remote(cot_hbm, cotb.at[zr], z_peer(k)) for k in (2, 6)}
    r_kv = {k: send_kv(y_peer(k)) for k in (1, 3)}
    w_rows = pl.ds(pl.multiple_of(core * 64, 64), 64)
    wp_rows = pl.ds(pl.multiple_of(HD + core * 64, 64), 64)
    r_w = remote(w_hbm.at[w_rows, other_cols], wp.at[wp_rows], cross)
    r_q = [remote(vqkv.at[0], q.at[xv], partner), remote(aqkv.at[0], q.at[xa], partner)]
    for k in (3, 5, 1, 7):
        r_cot[k] = remote(cot_hbm, cotb.at[zr], z_peer(k))
    r_sib = send_kv(sibling)
    r_ga = remote(acot_hbm, gb.at[xa], partner)

    rate = slope_ref[0] * LOG2E
    low1 = low_half(1)
    lane = lax.broadcasted_iota(jnp.int32, (1, QV), 1)
    lane_slot = lax.shift_right_logical(lane, 7)
    lane_frame = lax.shift_right_logical(lane, 6) - 2 * lane_slot
    query_frame_v = (8 * y + 4 * lane_slot + 2 * core + lane_frame).astype(F32)
    first = frame_ref[pl.ds(2 * y, 1), :].astype(F32)
    second = frame_ref[pl.ds(2 * y + 1, 1), :].astype(F32)
    query_frame_a = jnp.where(
        core == 0,
        jnp.where(low1, first, roll64(second)),
        jnp.where(low1, roll64(first), second),
    )
    row_frame = lax.shift_right_logical(lax.broadcasted_iota(jnp.int32, (TV, 1), 0), 6)
    for slot in range(NY):
        one = frame_ref[pl.ds(2 * slot + x_hi, 1), :].astype(F32)
        turned = jnp.broadcast_to(one, (128, 128)).T
        for c in range(2):
            frame_v = (8 * slot + 4 * x_hi + 2 * c + row_frame).astype(F32)
            bias_v[NY * c + slot] = rate * jnp.abs(frame_v - query_frame_a)
            frame_a = turned[64 * c : 64 * (c + 1), 0:1]
            bias_a[NY * c + slot] = rate * jnp.abs(frame_a - query_frame_v)

    r_kv[2] = []
    for part, k in ((0, 1), (1, 3)):
        for copy in r_kv[k]:
            copy.wait_recv()
        at = NY * core + y_slot(NY - k)
        r_kv[2].append(remote(kv.at[part, at], kv.at[part, at], y_peer(k)))
        r_sib.append(remote(kv.at[:, at], kv.at[:, at], sibling))
    r_far = []
    for k, half in ((2, 0), (6, 1)):
        r_cot[k].wait_recv()
        rows = pl.ds(pl.multiple_of(z_slot(NZ - k) * COLS + half * 96, 32), 96)
        r_far.append(remote(cotb.at[rows], cotb.at[rows], z_peer(k)))
    l_w.wait()
    wpt[:, 0:HD] = wp[0:HD, :].T
    r_w.wait_recv()
    r_w2 = remote(wp.at[wp_rows], wp.at[wp_rows], sibling)
    for copy in r_kv[2]:
        copy.wait_recv()
    at = NY * core + y_slot(2)
    r_sib.append(remote(kv.at[:, at], kv.at[:, at], sibling))

    l_kvv.wait()
    l_kva.wait()
    l_qv.wait()
    l_qa.wait()
    for copy in r_q + r_sib:
        copy.wait_recv()
    c2 = HD ** (-0.5) * LOG2E
    keys = kv[0].reshape(NS * TT, HD)
    values_t = kv[1].reshape(NS * TT, HD).T
    for c, cols in enumerate((slice(0, QV), slice(QV, QT))):
        wide = cols.stop - cols.start
        scores = (mm(keys, q[cols, :], NT) * c2).reshape(NS, TT, wide)
        part_v, part_a = scores[:, 0:TV], scores[:, TV:TT]
        if c == 0:
            part_a = part_a - bias_a[...]
        else:
            part_v = part_v - bias_v[...]
        high = jnp.maximum(
            jnp.max(part_v.reshape(NS * TV, wide), axis=0, keepdims=True),
            jnp.max(part_a.reshape(NS * TA, wide), axis=0, keepdims=True),
        )
        part_v = jnp.exp2(part_v - high)
        part_a = jnp.exp2(part_a - high)
        total = jnp.sum(part_v.reshape(NS * TV, wide), axis=0, keepdims=True) + jnp.sum(
            part_a.reshape(NS * TA, wide), axis=0, keepdims=True
        )
        p_scr[:, 0:TV, cols] = part_v
        p_scr[:, TV:TT, cols] = part_a
        probs = jnp.concatenate([part_v, part_a], axis=1).reshape(NS * TT, wide).astype(BF)
        mixed = mm(values_t, probs).T.astype(BF)
        rows_each = wide // 2
        for owner in range(2):
            piece = mixed[rows_each * owner : rows_each * (owner + 1)]
            if c == 0:
                osend[owner, 0:TV] = piece
            else:
                osend[owner, TV:TT] = piece
        if c == 0:
            sv_send[0:1, :] = high
            sv_send[1:2, :] = total
            r_sv = [
                remote(sv_send, sv_recv.at[n], to) for n, to in enumerate((partner, cross, corner))
            ]
            r_o = [
                remote(osend.at[1 - x_hi, 0:TV], orecv.at[0:TV], partner),
                remote(osend.at[x_hi, 0:TV], oc_recv, cross),
                remote(osend.at[1 - x_hi, 0:TV], od_recv, corner),
            ]
        else:
            sa_send[0:1, :] = high
            sa_send[1:2, :] = total
            r_sa = remote(sa_send, sa_recv, partner)
            r_oa = remote(osend.at[1 - x_hi, TV:TT], orecv.at[TV:TT], partner)

    l_cot.wait()
    for k in (3, 5, 1, 7):
        r_cot[k].wait_recv()
    for copy in r_far:
        copy.wait_recv()
    r_w2.wait_recv()
    cot_all = cotb[...]
    gp_send[...] = mm(wp[HD : 2 * HD, :], cot_all).astype(BF)
    r_gp = remote(gp_send, gp_recv, cross)
    r_gd = remote(gp_send, gd_recv, corner)
    go_send[...] = mm(wp[0:HD, :], cot_all).astype(BF)
    r_go = remote(go_send, go_recv, partner)
    wpt[:, HD : 2 * HD] = wp[HD : 2 * HD, :].T

    for copy in r_sv:
        copy.wait_recv()

    def shares(first, second):
        top = jnp.maximum(first[0:1, :], second[0:1, :])
        e_first = jnp.exp2(first[0:1, :] - top)
        e_second = jnp.exp2(second[0:1, :] - top)
        norm = first[1:2, :] * e_first + second[1:2, :] * e_second
        return e_first / norm, e_second / norm

    own_v, other_v = shares(sv_send, sv_recv[0])
    col_scr[0:1, 0:QV] = own_v
    col_scr[1:2, 0:QV] = other_v
    cross_v, corner_v = shares(sv_recv[1], sv_recv[2])
    col_scr[2:3, 0:QV] = cross_v
    col_scr[3:4, 0:QV] = corner_v

    pad = jnp.zeros((120, 128), F32)
    turned_v = jnp.concatenate([col_scr[:, xv], pad], axis=0).T
    for copy in r_o:
        copy.wait_recv()
    mine, other = osend[x_hi, 0:TV].astype(F32), orecv[0:TV].astype(F32)
    mix_vb = (mine * turned_v[:, 0:1] + other * turned_v[:, 1:2]).astype(BF)
    mix_c = oc_recv[...].astype(F32) * turned_v[:, 2:3] + od_recv[...].astype(F32) * turned_v[:, 3:4]

    both = jnp.concatenate([mix_vb, mix_c.astype(BF)], axis=1)
    os[...] = mm(wpt[...], both, NT).astype(BF).reshape(NZ, COLS, HD)
    r_ofar = [
        remote(os.at[z_slot(4), 96 * half : 96 * (half + 1)], ofar_recv.at[half], z_peer(k))
        for k, half in ((2, 0), (6, 1))
    ]
    r_os = {k: remote(os.at[z_slot(k)], orx.at[k - 1], z_peer(k)) for k in (3, 5, 1, 7)}

    r_gp.wait_recv()
    grad_t = (go_send[...].astype(F32) + gp_recv[...].astype(F32)).astype(BF).astype(F32)
    gb[xv, :] = grad_t.T.astype(BF)
    r_go.wait_recv()
    r_gd.wait_recv()
    grad_o = go_recv[...].astype(F32) + gd_recv[...].astype(F32)
    xv_other = pl.ds(pl.multiple_of((1 - x_hi) * TV, TV), TV)
    gb[xv_other, :] = grad_o.T.astype(BF)

    r_sa.wait_recv()
    own_a, other_a = shares(sa_send, sa_recv)
    own_factor = jnp.concatenate([own_v, own_a], axis=1)
    col_scr[0:1, QV:QT] = own_a
    col_scr[1:2, QV:QT] = other_a
    turned_a = jnp.concatenate([col_scr[:, QV:QT], pad], axis=0).T
    turned_a = jnp.where(x_hi == 1, turned_a[64:128], turned_a[0:64])
    r_oa.wait_recv()
    mine, other = osend[x_hi, TV:TT].astype(F32), orecv[TV:TT].astype(F32)
    mix_ab = (mine * turned_a[:, 0:1] + other * turned_a[:, 1:2]).astype(BF)
    res_ref[COLS : COLS + TA, :] = mix_ab
    l_ga.wait()
    dot_a = jnp.sum(
        jnp.concatenate(
            [gb[xa, :].astype(F32) * mix_ab.astype(F32), jnp.zeros((64, 128), F32)], axis=0
        ).T,
        axis=0,
        keepdims=True,
    )
    dot_v = jnp.sum(grad_t * mix_vb.astype(F32).T, axis=0, keepdims=True)
    dot_buf[x_hi, 0:1, 0:128] = dot_v
    dot_buf[x_hi, 0:1, 128:256] = dot_a
    r_dot = remote(dot_buf.at[x_hi], dot_buf.at[x_hi], partner)

    r_ga.wait_recv()
    order = ((0, 2), (0, 1), (0, 3), (0, 0), (1, 2), (1, 1), (1, 3), (1, 0))
    r_half, r_dkv = {}, []

    def hand_over(part, mine, k, value):
        if not mine:
            sib_send[k, part] = value.astype(BF)
            r_half[part, k] = remote(sib_send.at[k, part], sib_recv.at[k, part], sibling)
        elif k:
            r_half[part, k].wait_recv()
            dkv_send[k - 1, part] = (value + sib_recv[k, part].astype(F32)).astype(BF)
            r_dkv.append(
                remote(dkv_send.at[k - 1, part], dkv_recv.at[k - 1, part], y_peer(k))
            )
        else:
            dkv_own[part] = value

    def slot_of(mine, k):
        return NY * (core if mine else 1 - core) + y_slot(k)

    for mine, k in order:
        slot = slot_of(mine, k)
        prob = p_scr[slot] * own_factor
        p_scr[slot] = prob
        hand_over(1, mine, k, mm(prob.astype(BF), gb[...]))

    for at, half in ((2, 0), (6, 1)):
        r_ofar[half].wait_recv()
        rows = slice(96 * half, 96 * (half + 1))
        share = os[z_slot(at), rows].astype(F32) + ofar_recv[half].astype(F32)
        ofar[half, rows] = share.astype(BF)
        rest = slice(96 * (1 - half), 96 * (2 - half))
        ofar[half, rest] = os[z_slot(at), rest]
        r_os[at] = remote(ofar.at[half], orx.at[at - 1], z_peer(at))

    r_dot.wait_recv()
    dots = [dot_buf[k, 0:1, :] for k in range(2)]
    dot = jnp.concatenate(
        [dots[0][:, 0:128], dots[1][:, 0:128]]
        + [jnp.where(low1, dots[0][:, 128:256], roll64(dots[1][:, 128:256]))],
        axis=1,
    )
    c = HD ** (-0.5)
    dq_t = jnp.zeros((HD, QT), F32)
    for mine, k in order:
        slot = slot_of(mine, k)
        dp = mm(kv[1, slot], gb[...], NT)
        ds = (p_scr[slot] * (dp - dot)).astype(BF)
        hand_over(0, mine, k, mm(ds, q[...]) * c)
        dq_t = dq_t + mm(kv[0, slot].T, ds)
    dq = (dq_t * c).T.astype(BF)
    for owner in range(2):
        dq_send[owner, 0:TV] = dq[TV * owner : TV * (owner + 1)]
        dq_send[owner, TV:TT] = dq[QV + TA * owner : QV + TA * (owner + 1)]
    r_dq = remote(dq_send.at[1 - x_hi], dq_recv, partner)

    total = os[z].astype(F32)
    for k in (3, 5, 1, 7, 2, 6):
        r_os[k].wait_recv()
        total = total + orx[k - 1].astype(F32)
    res_ref[0:COLS, :] = total.astype(BF)
    r_half[0, 0].wait_recv()
    r_half[1, 0].wait_recv()
    dkv = dkv_own[...] + sib_recv[0].astype(F32)
    for copy in r_dkv:
        copy.wait_recv()
    for k in range(3):
        dkv = dkv + dkv_recv[k].astype(F32)
    dkv = dkv.astype(BF)
    for n in range(2):
        res_ref[AT_V + TV * (n + 1) : AT_V + TV * (n + 2), :] = dkv[n, 0:TV]
        res_ref[AT_A + TA * (n + 1) : AT_A + TA * (n + 2), :] = dkv[n, TV:TT]
    r_dq.wait_recv()
    dq = (dq_send[x_hi].astype(F32) + dq_recv[...].astype(F32)).astype(BF)
    res_ref[AT_V : AT_V + TV, :] = dq[0:TV]
    res_ref[AT_A : AT_A + TA, :] = dq[TV:TT]
    for copy in sends:
        copy.wait_send()


def unpack(res, out_ref, amix_ref, vgrad_ref, agrad_ref):
    out_ref[...] = res[0:COLS, :]
    amix_ref[...] = res[COLS : COLS + TA, :]
    vgrad_ref[...] = res[AT_V:AT_A, :].reshape(3, TV, HD)
    agrad_ref[...] = res[AT_A : AT_A + 3 * TA, :].reshape(3, TA, HD)


def per_device(video_qkv, audio_qkv, head_slopes, audio_frame, out_weight, video_cot, audio_cot):
    any_spec = pl.BlockSpec(memory_space=pl.ANY)
    vmem = pl.BlockSpec(memory_space=pltpu.VMEM)
    smem = pl.BlockSpec(memory_space=pltpu.SMEM)
    scratch = [
        pltpu.VMEM((2, NS, TT, HD), BF),
        pltpu.VMEM((QT, HD), BF),
        pltpu.VMEM((QT, HD), BF),
        pltpu.VMEM((HALF, TV), BF),
        pltpu.VMEM((2 * HD, HALF), BF),
        pltpu.VMEM((HALF, 2 * HD), BF),
        pltpu.VMEM((NS, TV, QA), F32),
        pltpu.VMEM((NS, TA, QV), F32),
        pltpu.VMEM((NS, TT, QT), F32),
        pltpu.VMEM((2, TT, HD), BF),
        pltpu.VMEM((TT, HD), BF),
        pltpu.VMEM((TV, HD), BF),
        pltpu.VMEM((TV, HD), BF),
        pltpu.VMEM((8, QV), F32),
        pltpu.VMEM((3, 8, QV), F32),
        pltpu.VMEM((8, QA), F32),
        pltpu.VMEM((8, QA), F32),
        pltpu.VMEM((8, QT), F32),
        pltpu.VMEM((HD, TV), BF),
        pltpu.VMEM((HD, TV), BF),
        pltpu.VMEM((HD, TV), BF),
        pltpu.VMEM((HD, TV), BF),
        pltpu.VMEM((HD, TV), BF),
        pltpu.VMEM((2, 8, 256), F32),
        pltpu.VMEM((NZ, COLS, HD), BF),
        pltpu.VMEM((NZ - 1, COLS, HD), BF),
        pltpu.VMEM((2, COLS, HD), BF),
        pltpu.VMEM((2, COLS // 2, HD), BF),
        pltpu.VMEM((NY, 2, TT, HD), BF),
        pltpu.VMEM((NY, 2, TT, HD), BF),
        pltpu.VMEM((3, 2, TT, HD), BF),
        pltpu.VMEM((3, 2, TT, HD), BF),
        pltpu.VMEM((2, TT, HD), F32),
        pltpu.VMEM((2, TT, HD), BF),
        pltpu.VMEM((TT, HD), BF),
        pltpu.SemaphoreType.DMA((8,)),
        pltpu.SemaphoreType.DMA((64,)),
        pltpu.SemaphoreType.DMA((64,)),
    ]
    res = pl.pallas_call(
        kernel,
        out_shape=jax.ShapeDtypeStruct((AT_A + 3 * TA, HD), BF),
        in_specs=[any_spec, any_spec, smem, vmem, any_spec, any_spec, any_spec],
        out_specs=vmem,
        scratch_shapes=scratch,
        compiler_params=pltpu.CompilerParams(
            collective_id=0, has_side_effects=True, vmem_limit_bytes=56 * 1024 * 1024
        ),
    )(
        video_qkv,
        audio_qkv,
        head_slopes,
        audio_frame.reshape(8, 128),
        out_weight,
        video_cot.T,
        audio_cot,
    )
    out_t, audio_mix, video_grad, audio_grad = pl.pallas_call(
        unpack,
        out_shape=(
            jax.ShapeDtypeStruct((COLS, TV), BF),
            jax.ShapeDtypeStruct((TA, HD), BF),
            jax.ShapeDtypeStruct((3, TV, HD), BF),
            jax.ShapeDtypeStruct((3, TA, HD), BF),
        ),
        in_specs=[vmem],
        out_specs=(vmem,) * 4,
    )(res)
    return out_t.T, audio_mix, video_grad, audio_grad


def solution(mesh):
    in_specs = (
        P(None, "seq", "grp"),
        P(None, "seq", "grp"),
        P("grp"),
        P(),
        P("grp", None),
        P("seq", "grp"),
        P("seq", "grp"),
    )
    out_specs = (P("seq", "grp"), P("seq", "grp"), P(None, "seq", "grp"), P(None, "seq", "grp"))
    return jax.shard_map(
        per_device, mesh=mesh, in_specs=in_specs, out_specs=out_specs, check_vma=False
    )
```

```python
import math

import jax
import jax.numpy as jnp
from jax import lax
from jax.experimental import pallas as pl
from jax.experimental.pallas import tpu as pltpu
from jax.sharding import PartitionSpec as P

BF = jnp.bfloat16
F32 = jnp.float32
HD = 128
TV = 128
TA = 64
TT = TV + TA
NY = 4
NS = 2 * NY
NZ = 8
QV = 2 * TV
QA = 2 * TA
QT = QV + QA
COLS = 192
HALF = NZ * COLS
LOG2E = 1.4426950408889634
AT_V = COLS + TA
AT_A = AT_V + 3 * TV

NN = (((1,), (0,)), ((), ()))
NT = (((1,), (1,)), ((), ()))


def mm(a, b, dims=NN):
    return lax.dot_general(a, b, dims, preferred_element_type=F32)


def roll64(x):
    return pltpu.roll(x, 64, 1)


def low_half(rows):
    return lax.broadcasted_iota(jnp.int32, (rows, 128), 1) < 64


def kernel(
    vqkv, aqkv, slope_ref, frame_ref, w_hbm, cot_hbm, acot_hbm,
    res_ref,
    kv, q, gb, cotb, wp, wpt, bias_v, bias_a, p_scr,
    osend, orecv, oc_recv, od_recv, sv_send, sv_recv, sa_send, sa_recv, col_scr,
    gp_send, gp_recv, go_send, go_recv, gd_recv, dot_buf, os, orx, ofar, ofar_recv,
    sib_send, sib_recv, dkv_send, dkv_recv, dkv_own, dq_send, dq_recv,
    lsem, ssem, rsem,
):
    s = lax.axis_index("seq")
    grp = lax.axis_index("grp")
    y = lax.div(s, 4)
    x_hi = lax.div(lax.rem(s, 4), 2)
    core = lax.rem(s, 2)
    x_lo = lax.div(grp, NZ)
    z = lax.rem(grp, NZ)
    sibling = (s + 1 - 2 * core, grp)
    partner = (s + 2 - 4 * x_hi, grp)
    cross = (s, lax.rem(grp + NZ, 2 * NZ))
    corner = (s + 2 - 4 * x_hi, lax.rem(grp + NZ, 2 * NZ))

    def y_slot(k):
        return lax.rem(y + k, NY)

    def y_peer(k):
        return (lax.rem(s + 4 * k, 4 * NY), grp)

    def z_slot(k):
        return lax.rem(z + k, NZ)

    def z_peer(k):
        return (s, x_lo * NZ + z_slot(k))

    sends = []
    count = [0]

    def remote(src, dst, to):
        i = count[0]
        count[0] += 1
        copy = pltpu.make_async_remote_copy(
            src_ref=src,
            dst_ref=dst,
            send_sem=ssem.at[i],
            recv_sem=rsem.at[i],
            device_id=to,
            device_id_type=pl.DeviceIdType.MESH,
        )
        copy.start()
        sends.append(copy)
        return copy

    local_count = [0]

    def local(src, dst):
        i = local_count[0]
        local_count[0] += 1
        copy = pltpu.make_async_copy(src, dst, lsem.at[i])
        copy.start()
        return copy

    barrier = pltpu.get_barrier_semaphore()
    peers = (
        [z_peer(k) for k in range(1, NZ)]
        + [cross, corner, sibling, partner]
        + [y_peer(k) for k in range(1, NY)]
    )
    for peer in peers:
        pl.semaphore_signal(barrier, inc=1, device_id=peer, device_id_type=pl.DeviceIdType.MESH)

    xv = pl.ds(pl.multiple_of(x_hi * TV, TV), TV)
    xa = pl.ds(pl.multiple_of(QV + x_hi * TA, TA), TA)
    zr = pl.ds(pl.multiple_of(z * COLS, 64), COLS)
    own_cols = pl.ds(pl.multiple_of(x_lo * HALF, HALF), HALF)
    other_cols = pl.ds(pl.multiple_of((1 - x_lo) * HALF, HALF), HALF)
    slot_own = NY * core + y
    l_cot = local(cot_hbm, cotb.at[zr])
    l_w = local(w_hbm.at[:, own_cols], wp.at[0:HD])
    l_kvv = local(vqkv.at[1:3], kv.at[:, slot_own, 0:TV])
    l_kva = local(aqkv.at[1:3], kv.at[:, slot_own, TV:TT])
    l_qv = local(vqkv.at[0], q.at[xv])
    l_qa = local(aqkv.at[0], q.at[xa])
    l_ga = local(acot_hbm, gb.at[xa])

    pl.semaphore_wait(barrier, len(peers))

    def send_kv(to):
        return [
            remote(vqkv.at[1:3], kv.at[:, slot_own, 0:TV], to),
            remote(aqkv.at[1:3], kv.at[:, slot_own, TV:TT], to),
        ]

    r_cot = {k: remote(cot_hbm, cotb.at[zr], z_peer(k)) for k in (2, 6)}
    r_kv = {k: send_kv(y_peer(k)) for k in (2, 1, 3)}
    w_rows = pl.ds(pl.multiple_of(core * 64, 64), 64)
    wp_rows = pl.ds(pl.multiple_of(HD + core * 64, 64), 64)
    r_w = remote(w_hbm.at[w_rows, other_cols], wp.at[wp_rows], cross)
    r_q = [remote(vqkv.at[0], q.at[xv], partner), remote(aqkv.at[0], q.at[xa], partner)]
    for k in (3, 5, 1, 7):
        r_cot[k] = remote(cot_hbm, cotb.at[zr], z_peer(k))
    r_sib = send_kv(sibling)
    r_ga = remote(acot_hbm, gb.at[xa], partner)

    rate = slope_ref[0] * LOG2E
    low1 = low_half(1)
    lane = lax.broadcasted_iota(jnp.int32, (1, QV), 1)
    lane_slot = lax.shift_right_logical(lane, 7)
    lane_frame = lax.shift_right_logical(lane, 6) - 2 * lane_slot
    query_frame_v = (8 * y + 4 * lane_slot + 2 * core + lane_frame).astype(F32)
    first = frame_ref[pl.ds(2 * y, 1), :].astype(F32)
    second = frame_ref[pl.ds(2 * y + 1, 1), :].astype(F32)
    query_frame_a = jnp.where(
        core == 0,
        jnp.where(low1, first, roll64(second)),
        jnp.where(low1, roll64(first), second),
    )
    row_frame = lax.shift_right_logical(lax.broadcasted_iota(jnp.int32, (TV, 1), 0), 6)
    for slot in range(NY):
        one = frame_ref[pl.ds(2 * slot + x_hi, 1), :].astype(F32)
        turned = jnp.broadcast_to(one, (128, 128)).T
        for c in range(2):
            frame_v = (8 * slot + 4 * x_hi + 2 * c + row_frame).astype(F32)
            bias_v[NY * c + slot] = rate * jnp.abs(frame_v - query_frame_a)
            frame_a = turned[64 * c : 64 * (c + 1), 0:1]
            bias_a[NY * c + slot] = rate * jnp.abs(frame_a - query_frame_v)

    for k in (1, 3):
        for copy in r_kv[k]:
            copy.wait_recv()
        at = NY * core + y_slot(NY - k)
        r_sib.append(remote(kv.at[:, at], kv.at[:, at], sibling))
    r_far = []
    for k, half in ((2, 0), (6, 1)):
        r_cot[k].wait_recv()
        rows = pl.ds(pl.multiple_of(z_slot(NZ - k) * COLS + half * 96, 32), 96)
        r_far.append(remote(cotb.at[rows], cotb.at[rows], z_peer(k)))
    l_w.wait()
    wpt[:, 0:HD] = wp[0:HD, :].T
    r_w.wait_recv()
    r_w2 = remote(wp.at[wp_rows], wp.at[wp_rows], sibling)
    for copy in r_kv[2]:
        copy.wait_recv()
    at = NY * core + y_slot(2)
    r_sib.append(remote(kv.at[:, at], kv.at[:, at], sibling))

    l_kvv.wait()
    l_kva.wait()
    l_qv.wait()
    l_qa.wait()
    for copy in r_q + r_sib:
        copy.wait_recv()
    c2 = HD ** (-0.5) * LOG2E
    keys = kv[0].reshape(NS * TT, HD)
    values_t = kv[1].reshape(NS * TT, HD).T
    for c, cols in enumerate((slice(0, QV), slice(QV, QT))):
        wide = cols.stop - cols.start
        scores = (mm(keys, q[cols, :], NT) * c2).reshape(NS, TT, wide)
        part_v, part_a = scores[:, 0:TV], scores[:, TV:TT]
        if c == 0:
            part_a = part_a - bias_a[...]
        else:
            part_v = part_v - bias_v[...]
        high = jnp.maximum(
            jnp.max(part_v.reshape(NS * TV, wide), axis=0, keepdims=True),
            jnp.max(part_a.reshape(NS * TA, wide), axis=0, keepdims=True),
        )
        part_v = jnp.exp2(part_v - high)
        part_a = jnp.exp2(part_a - high)
        total = jnp.sum(part_v.reshape(NS * TV, wide), axis=0, keepdims=True) + jnp.sum(
            part_a.reshape(NS * TA, wide), axis=0, keepdims=True
        )
        p_scr[:, 0:TV, cols] = part_v
        p_scr[:, TV:TT, cols] = part_a
        probs = jnp.concatenate([part_v, part_a], axis=1).reshape(NS * TT, wide).astype(BF)
        mixed = mm(values_t, probs).T.astype(BF)
        rows_each = wide // 2
        for owner in range(2):
            piece = mixed[rows_each * owner : rows_each * (owner + 1)]
            if c == 0:
                osend[owner, 0:TV] = piece
            else:
                osend[owner, TV:TT] = piece
        if c == 0:
            sv_send[0:1, :] = high
            sv_send[1:2, :] = total
            r_sv = [
                remote(sv_send, sv_recv.at[n], to) for n, to in enumerate((partner, cross, corner))
            ]
            r_o = [
                remote(osend.at[1 - x_hi, 0:TV], orecv.at[0:TV], partner),
                remote(osend.at[x_hi, 0:TV], oc_recv, cross),
                remote(osend.at[1 - x_hi, 0:TV], od_recv, corner),
            ]
        else:
            sa_send[0:1, :] = high
            sa_send[1:2, :] = total
            r_sa = remote(sa_send, sa_recv, partner)
            r_oa = remote(osend.at[1 - x_hi, TV:TT], orecv.at[TV:TT], partner)

    l_cot.wait()
    for k in (3, 5, 1, 7):
        r_cot[k].wait_recv()
    for copy in r_far:
        copy.wait_recv()
    r_w2.wait_recv()
    cot_all = cotb[...]
    gp_send[...] = mm(wp[HD : 2 * HD, :], cot_all).astype(BF)
    r_gp = remote(gp_send, gp_recv, cross)
    r_gd = remote(gp_send, gd_recv, corner)
    go_send[...] = mm(wp[0:HD, :], cot_all).astype(BF)
    r_go = remote(go_send, go_recv, partner)
    wpt[:, HD : 2 * HD] = wp[HD : 2 * HD, :].T

    for copy in r_sv:
        copy.wait_recv()

    def shares(first, second):
        top = jnp.maximum(first[0:1, :], second[0:1, :])
        e_first = jnp.exp2(first[0:1, :] - top)
        e_second = jnp.exp2(second[0:1, :] - top)
        norm = first[1:2, :] * e_first + second[1:2, :] * e_second
        return e_first / norm, e_second / norm

    own_v, other_v = shares(sv_send, sv_recv[0])
    col_scr[0:1, 0:QV] = own_v
    col_scr[1:2, 0:QV] = other_v
    cross_v, corner_v = shares(sv_recv[1], sv_recv[2])
    col_scr[2:3, 0:QV] = cross_v
    col_scr[3:4, 0:QV] = corner_v

    pad = jnp.zeros((120, 128), F32)
    turned_v = jnp.concatenate([col_scr[:, xv], pad], axis=0).T
    for copy in r_o:
        copy.wait_recv()
    mine, other = osend[x_hi, 0:TV].astype(F32), orecv[0:TV].astype(F32)
    mix_vb = (mine * turned_v[:, 0:1] + other * turned_v[:, 1:2]).astype(BF)
    mix_c = oc_recv[...].astype(F32) * turned_v[:, 2:3] + od_recv[...].astype(F32) * turned_v[:, 3:4]

    both = jnp.concatenate([mix_vb, mix_c.astype(BF)], axis=1)
    os[...] = mm(wpt[...], both, NT).astype(BF).reshape(NZ, COLS, HD)
    r_ofar = [
        remote(os.at[z_slot(4), 96 * half : 96 * (half + 1)], ofar_recv.at[half], z_peer(k))
        for k, half in ((2, 0), (6, 1))
    ]
    r_os = {k: remote(os.at[z_slot(k)], orx.at[k - 1], z_peer(k)) for k in (3, 5, 1, 7)}

    r_gp.wait_recv()
    grad_t = (go_send[...].astype(F32) + gp_recv[...].astype(F32)).astype(BF).astype(F32)
    gb[xv, :] = grad_t.T.astype(BF)
    r_go.wait_recv()
    r_gd.wait_recv()
    grad_o = go_recv[...].astype(F32) + gd_recv[...].astype(F32)
    xv_other = pl.ds(pl.multiple_of((1 - x_hi) * TV, TV), TV)
    gb[xv_other, :] = grad_o.T.astype(BF)

    r_sa.wait_recv()
    own_a, other_a = shares(sa_send, sa_recv)
    own_factor = jnp.concatenate([own_v, own_a], axis=1)
    col_scr[0:1, QV:QT] = own_a
    col_scr[1:2, QV:QT] = other_a
    turned_a = jnp.concatenate([col_scr[:, QV:QT], pad], axis=0).T
    turned_a = jnp.where(x_hi == 1, turned_a[64:128], turned_a[0:64])
    r_oa.wait_recv()
    mine, other = osend[x_hi, TV:TT].astype(F32), orecv[TV:TT].astype(F32)
    mix_ab = (mine * turned_a[:, 0:1] + other * turned_a[:, 1:2]).astype(BF)
    res_ref[COLS : COLS + TA, :] = mix_ab
    l_ga.wait()
    dot_a = jnp.sum(
        jnp.concatenate(
            [gb[xa, :].astype(F32) * mix_ab.astype(F32), jnp.zeros((64, 128), F32)], axis=0
        ).T,
        axis=0,
        keepdims=True,
    )
    dot_v = jnp.sum(grad_t * mix_vb.astype(F32).T, axis=0, keepdims=True)
    dot_buf[x_hi, 0:1, 0:128] = dot_v
    dot_buf[x_hi, 0:1, 128:256] = dot_a
    r_dot = remote(dot_buf.at[x_hi], dot_buf.at[x_hi], partner)

    r_ga.wait_recv()
    order = ((0, 2), (0, 1), (0, 3), (0, 0), (1, 2), (1, 1), (1, 3), (1, 0))
    r_half, r_dkv = {}, []

    def hand_over(part, mine, k, value):
        if not mine:
            sib_send[k, part] = value.astype(BF)
            r_half[part, k] = remote(sib_send.at[k, part], sib_recv.at[k, part], sibling)
        elif k:
            r_half[part, k].wait_recv()
            dkv_send[k - 1, part] = (value + sib_recv[k, part].astype(F32)).astype(BF)
            r_dkv.append(
                remote(dkv_send.at[k - 1, part], dkv_recv.at[k - 1, part], y_peer(k))
            )
        else:
            dkv_own[part] = value

    def slot_of(mine, k):
        return NY * (core if mine else 1 - core) + y_slot(k)

    for mine, k in order:
        slot = slot_of(mine, k)
        prob = p_scr[slot] * own_factor
        p_scr[slot] = prob
        hand_over(1, mine, k, mm(prob.astype(BF), gb[...]))

    for at, half in ((2, 0), (6, 1)):
        r_ofar[half].wait_recv()
        rows = slice(96 * half, 96 * (half + 1))
        share = os[z_slot(at), rows].astype(F32) + ofar_recv[half].astype(F32)
        ofar[half, rows] = share.astype(BF)
        rest = slice(96 * (1 - half), 96 * (2 - half))
        ofar[half, rest] = os[z_slot(at), rest]
        r_os[at] = remote(ofar.at[half], orx.at[at - 1], z_peer(at))

    r_dot.wait_recv()
    dots = [dot_buf[k, 0:1, :] for k in range(2)]
    dot = jnp.concatenate(
        [dots[0][:, 0:128], dots[1][:, 0:128]]
        + [jnp.where(low1, dots[0][:, 128:256], roll64(dots[1][:, 128:256]))],
        axis=1,
    )
    c = HD ** (-0.5)
    dq_t = jnp.zeros((HD, QT), F32)
    for mine, k in order:
        slot = slot_of(mine, k)
        dp = mm(kv[1, slot], gb[...], NT)
        ds = (p_scr[slot] * (dp - dot)).astype(BF)
        hand_over(0, mine, k, mm(ds, q[...]) * c)
        dq_t = dq_t + mm(kv[0, slot].T, ds)
    dq = (dq_t * c).T.astype(BF)
    for owner in range(2):
        dq_send[owner, 0:TV] = dq[TV * owner : TV * (owner + 1)]
        dq_send[owner, TV:TT] = dq[QV + TA * owner : QV + TA * (owner + 1)]
    r_dq = remote(dq_send.at[1 - x_hi], dq_recv, partner)

    total = os[z].astype(F32)
    for k in (3, 5, 1, 7, 2, 6):
        r_os[k].wait_recv()
        total = total + orx[k - 1].astype(F32)
    res_ref[0:COLS, :] = total.astype(BF)
    r_half[0, 0].wait_recv()
    r_half[1, 0].wait_recv()
    dkv = dkv_own[...] + sib_recv[0].astype(F32)
    for copy in r_dkv:
        copy.wait_recv()
    for k in range(3):
        dkv = dkv + dkv_recv[k].astype(F32)
    dkv = dkv.astype(BF)
    for n in range(2):
        res_ref[AT_V + TV * (n + 1) : AT_V + TV * (n + 2), :] = dkv[n, 0:TV]
        res_ref[AT_A + TA * (n + 1) : AT_A + TA * (n + 2), :] = dkv[n, TV:TT]
    r_dq.wait_recv()
    dq = (dq_send[x_hi].astype(F32) + dq_recv[...].astype(F32)).astype(BF)
    res_ref[AT_V : AT_V + TV, :] = dq[0:TV]
    res_ref[AT_A : AT_A + TA, :] = dq[TV:TT]
    for copy in sends:
        copy.wait_send()


def unpack(res, out_ref, amix_ref, vgrad_ref, agrad_ref):
    out_ref[...] = res[0:COLS, :]
    amix_ref[...] = res[COLS : COLS + TA, :]
    vgrad_ref[...] = res[AT_V:AT_A, :].reshape(3, TV, HD)
    agrad_ref[...] = res[AT_A : AT_A + 3 * TA, :].reshape(3, TA, HD)


def per_device(video_qkv, audio_qkv, head_slopes, audio_frame, out_weight, video_cot, audio_cot):
    any_spec = pl.BlockSpec(memory_space=pl.ANY)
    vmem = pl.BlockSpec(memory_space=pltpu.VMEM)
    smem = pl.BlockSpec(memory_space=pltpu.SMEM)
    scratch = [
        pltpu.VMEM((2, NS, TT, HD), BF),
        pltpu.VMEM((QT, HD), BF),
        pltpu.VMEM((QT, HD), BF),
        pltpu.VMEM((HALF, TV), BF),
        pltpu.VMEM((2 * HD, HALF), BF),
        pltpu.VMEM((HALF, 2 * HD), BF),
        pltpu.VMEM((NS, TV, QA), F32),
        pltpu.VMEM((NS, TA, QV), F32),
        pltpu.VMEM((NS, TT, QT), F32),
        pltpu.VMEM((2, TT, HD), BF),
        pltpu.VMEM((TT, HD), BF),
        pltpu.VMEM((TV, HD), BF),
        pltpu.VMEM((TV, HD), BF),
        pltpu.VMEM((8, QV), F32),
        pltpu.VMEM((3, 8, QV), F32),
        pltpu.VMEM((8, QA), F32),
        pltpu.VMEM((8, QA), F32),
        pltpu.VMEM((8, QT), F32),
        pltpu.VMEM((HD, TV), BF),
        pltpu.VMEM((HD, TV), BF),
        pltpu.VMEM((HD, TV), BF),
        pltpu.VMEM((HD, TV), BF),
        pltpu.VMEM((HD, TV), BF),
        pltpu.VMEM((2, 8, 256), F32),
        pltpu.VMEM((NZ, COLS, HD), BF),
        pltpu.VMEM((NZ - 1, COLS, HD), BF),
        pltpu.VMEM((2, COLS, HD), BF),
        pltpu.VMEM((2, COLS // 2, HD), BF),
        pltpu.VMEM((NY, 2, TT, HD), BF),
        pltpu.VMEM((NY, 2, TT, HD), BF),
        pltpu.VMEM((3, 2, TT, HD), BF),
        pltpu.VMEM((3, 2, TT, HD), BF),
        pltpu.VMEM((2, TT, HD), F32),
        pltpu.VMEM((2, TT, HD), BF),
        pltpu.VMEM((TT, HD), BF),
        pltpu.SemaphoreType.DMA((8,)),
        pltpu.SemaphoreType.DMA((64,)),
        pltpu.SemaphoreType.DMA((64,)),
    ]
    res = pl.pallas_call(
        kernel,
        out_shape=jax.ShapeDtypeStruct((AT_A + 3 * TA, HD), BF),
        in_specs=[any_spec, any_spec, smem, vmem, any_spec, any_spec, any_spec],
        out_specs=vmem,
        scratch_shapes=scratch,
        compiler_params=pltpu.CompilerParams(
            collective_id=0, has_side_effects=True, vmem_limit_bytes=56 * 1024 * 1024
        ),
    )(
        video_qkv,
        audio_qkv,
        head_slopes,
        audio_frame.reshape(8, 128),
        out_weight,
        video_cot.T,
        audio_cot,
    )
    out_t, audio_mix, video_grad, audio_grad = pl.pallas_call(
        unpack,
        out_shape=(
            jax.ShapeDtypeStruct((COLS, TV), BF),
            jax.ShapeDtypeStruct((TA, HD), BF),
            jax.ShapeDtypeStruct((3, TV, HD), BF),
            jax.ShapeDtypeStruct((3, TA, HD), BF),
        ),
        in_specs=[vmem],
        out_specs=(vmem,) * 4,
    )(res)
    return out_t.T, audio_mix, video_grad, audio_grad


def solution(mesh):
    in_specs = (
        P(None, "seq", "grp"),
        P(None, "seq", "grp"),
        P("grp"),
        P(),
        P("grp", None),
        P("seq", "grp"),
        P("seq", "grp"),
    )
    out_specs = (P("seq", "grp"), P("seq", "grp"), P(None, "seq", "grp"), P(None, "seq", "grp"))
    return jax.shard_map(
        per_device, mesh=mesh, in_specs=in_specs, out_specs=out_specs, check_vma=False
    )
```
